128 devices in a mesh: gx: 32 (over x, z, y_lo), gy: 4 (over y_hi, core).
Axes of the slice: x: 4, y: 4 (y_hi: 2, y_lo: 2; y = y_hi * 2 + y_lo), z: 4, core: 2. Of those that a mesh axis runs over, the one named last changes fastest.
Arguments:
- source_snaps: float32 [4, 1536, 64, 256], P(None, 'gx', 'gy'), may hold values from -6 to 6
- receiver_snaps: float32 [4, 1536, 64, 256], P(None, 'gx', 'gy'), may hold values from -6 to 6
- snap_pairs: int32 [3, 2], replicated, may hold values from 0 to 3
- offset_lags: int32 [17], replicated, may hold values from -24 to 24, as said below
- weight_table: float32 [4, 17], replicated, may hold values from 0.2 to 1
- weight_index: int32 [3], replicated, may hold values from 0 to 3
Outputs:
- adjoint_source: float32 [3, 1536, 64, 256], P(None, 'gx', 'gy')
- adjoint_receiver: float32 [3, 1536, 64, 256], P(None, 'gx', 'gy')
The draws below stay inside these ranges and needn't reach their ends.
Inputs may be any that keep to these rules, and one draw needn't show every extreme that they name: `offset_lags`: strictly increasing; the first entry is -24 and the last is 24.
All inputs are finite; a program needn't handle non-finite values.
Results may differ from the reference program's by a relative error of at most 0.00002.
Values sent between devices are 32-bit elements; how exact they have to be, the bound alone decides.
No kernel may reach another device: no remote copies, remote signals or barrier semaphores. Data moves between devices by JAX's collectives and lax.ppermute only.
A program may use at most 128 MiB of HBM per device.

```python
import jax
import jax.numpy as jnp
from jax import lax

NZ = 256
NSNAP = 4
PAIRS = 3
NOFF = 17
MAXLAG = 24
NW = 4
NX = 1536
NY = 64


def draw_offset_lags(key, part):
    ramp = jnp.arange(NOFF, dtype=jnp.int32)
    base = -MAXLAG + ramp * (2 * MAXLAG) // (NOFF - 1)
    jitter = jax.random.randint(key, (NOFF,), -1, 2, dtype=jnp.int32)
    inner = (ramp > 0) & (ramp < NOFF - 1)
    return (base + jnp.where(inner, jitter, 0)).astype(jnp.int32)


def with_ends(drawn, key, smallest, largest):
    extent = drawn.shape
    spot = [jax.random.randint(jax.random.fold_in(key, axis), (), 0, extent[axis]) for axis in range(len(extent))]
    drawn = drawn.at[tuple(spot)].set(smallest)
    longest = extent.index(max(extent))
    spot[longest] = (spot[longest] + 1) % extent[longest]
    return drawn.at[tuple(spot)].set(largest)


def shard_levels(rng, dims, split, least, high):
    def one(axis_at, parts):
        draws = jax.random.uniform(jax.random.fold_in(jax.random.fold_in(rng, 6), axis_at), (parts,), jnp.float32, least / len(split), high / len(split))
        return jnp.repeat(jnp.exp(draws), dims[axis_at] // parts).reshape((-1,) + (1,) * (len(dims) - axis_at - 1))

    factor_of = one(*split[0])
    for cut in split[1:]:
        factor_of = factor_of * one(*cut)
    return factor_of


def scatter_about(key, dims, deviation, most, cuts=(), held_as=jnp.bfloat16):
    values = jax.random.normal(key, dims, jnp.float32) * deviation
    if len(cuts) > 0:
        values = shard_levels(key, dims, cuts, -0.22, 0.18) * values
    return jnp.clip(values, min=-most, max=most).astype(held_as)


def setup_inputs(seed: int = 0) -> dict:
    keys = jax.random.split(jax.random.key(seed), 7)
    return {
        "source_snaps": scatter_about(keys[0], (NSNAP, NX, NY, NZ), 1.0, 6.0, ((1, 32), (2, 4)), jnp.float32),
        "receiver_snaps": scatter_about(keys[1], (NSNAP, NX, NY, NZ), 1.0, 6.0, ((1, 32), (2, 4)), jnp.float32),
        "snap_pairs": with_ends(jax.random.randint(keys[2], (PAIRS, 2), 0, NSNAP), jax.random.fold_in(keys[2], 1), 0, NSNAP - 1).astype(jnp.int32),
        "offset_lags": draw_offset_lags(jax.random.fold_in(keys[6], 71), 0),
        "weight_table": jnp.clip(jax.random.uniform(keys[4], (NW, NOFF), jnp.float32, 0.2, 1.0), 0.2, 1.0),
        "weight_index": jax.random.randint(keys[5], (PAIRS,), 0, NW).astype(jnp.int32),
    }


def smooth(values):
    return (values[:, :-4] + values[:, 4:] + 4.0 * (values[:, 1:-3] + values[:, 3:-1]) + 6.0 * values[:, 2:-2]) / 16.0


def reference(source_snaps, receiver_snaps, snap_pairs, offset_lags, weight_table, weight_index):
    source_list = []
    receiver_list = []
    for pair_index in range(PAIRS):
        source_field = source_snaps[snap_pairs[pair_index, 0]]
        receiver_field = receiver_snaps[snap_pairs[pair_index, 1]]
        source_pad = jnp.pad(source_field, ((2 * MAXLAG, 2 * MAXLAG), (2, 2), (0, 0)))
        receiver_pad = jnp.pad(receiver_field, ((2 * MAXLAG, 2 * MAXLAG), (2, 2), (0, 0)))
        weights = weight_table[weight_index[pair_index]]

        def step(offset, running):
            source_total, receiver_total = running
            offset_lag = offset_lags[offset]
            weight = weights[offset]
            shifted_source = lax.dynamic_slice_in_dim(source_pad, 2 * MAXLAG - offset_lag, NX, 0)
            shifted_receiver = lax.dynamic_slice_in_dim(receiver_pad, 2 * MAXLAG + offset_lag, NX, 0)
            smoothed = smooth(weight * shifted_source * shifted_receiver)
            smoothed_pad = jnp.pad(smoothed, ((MAXLAG, MAXLAG), (0, 0), (0, 0)))
            far_receiver = lax.dynamic_slice_in_dim(receiver_pad, 2 * MAXLAG + 2 * offset_lag, NX, 0)[:, 2:-2]
            far_source = lax.dynamic_slice_in_dim(source_pad, 2 * MAXLAG - 2 * offset_lag, NX, 0)[:, 2:-2]
            source_total = source_total + lax.dynamic_slice_in_dim(smoothed_pad, MAXLAG + offset_lag, NX, 0) * far_receiver
            receiver_total = receiver_total + lax.dynamic_slice_in_dim(smoothed_pad, MAXLAG - offset_lag, NX, 0) * far_source
            return (source_total, receiver_total)

        zeros = jnp.zeros(source_field.shape, jnp.float32)
        source_total, receiver_total = lax.fori_loop(0, NOFF, step, (zeros, zeros))
        source_list.append(source_total)
        receiver_list.append(receiver_total)
    return (jnp.stack(source_list), jnp.stack(receiver_list))
```

```python
import functools

import jax
import jax.numpy as jnp
from jax import lax
from jax.experimental import pallas as pl
from jax.experimental.pallas import tpu as pltpu
from jax.sharding import PartitionSpec as P

F32 = jnp.float32


def moves(mesh):
    nx, ny = mesh.shape["gx"], mesh.shape["gy"]
    flat = lambda x, y: x * ny + y
    middle = [y for y in range(ny) if y not in (0, ny - 1)]
    across = [(x, x ^ 1) for x in range(nx) if x ^ 1 < nx]
    onward = [(x, x + 2) for x in range(0, nx - 2, 2)] + [(x, x - 2) for x in range(3, nx, 2)]
    whole = lambda route, rows: [(flat(a, y), flat(b, y)) for a, b in route for y in rows]
    twins = [(flat(x, y), flat(x, y ^ 1)) for x in range(nx) for y in range(ny)]
    seam = [(flat(x, a), flat(x, b)) for x in range(nx) for y in range(1, ny - 1, 2) for a, b in ((y, y + 1), (y + 1, y))]
    return {
        "across": whole(across, range(ny)),
        "onward": whole(onward, range(ny)),
        "across_edge": whole(across, middle),
        "onward_edge": whole(onward, middle),
        "twins": twins,
        "seam": seam,
    }


def image_kernel(
    place, lags, weights, user, own, near, far, own_twin, own_edge, near_twin, near_edge, far_twin, far_edge,
    mate, mate_twin, mate_edge, out, ext, prod, mix, mext, done, sems,
):
    cells, rows, _ = own.shape
    odd, second = place[0], place[1]
    near_at = jnp.where(odd == 1, 0, 2 * cells)
    far_at = jnp.where(odd == 1, 2 * cells, 0)
    spots = ((own, cells, own_twin, own_edge), (near, near_at, near_twin, near_edge), (far, far_at, far_twin, far_edge))

    def fill(index, block, target, at):
        return pltpu.make_async_copy(block, target.at[pl.ds(at, cells), pl.ds(8, rows)], sems.at[index])

    copies = [fill(i, spot[0], ext, spot[1]) for i, spot in enumerate(spots)] + [fill(3, mate, mext, 0)]
    for copy in copies:
        copy.start()
    low_tile = lax.broadcasted_iota(jnp.int32, (8, ext.shape[2]), 0)

    def edges(x, twin, edge):
        t, e = twin[x], edge[x]
        return jnp.where(second == 1, t, e), jnp.where(second == 1, e, t)

    for i, (_, at, twin, edge) in enumerate(spots):
        copies[i].wait()

        def product(x, carry):
            low, high = edges(x, twin, edge)
            ext[at + x, 6:8] = low
            ext[at + x, rows + 8 : rows + 10] = high
            here = ext[at + x, 8 : rows + 8]
            prod[at + x, 0:rows] = here * here
            prod[at + x, rows : 2 * rows] = here * ext[at + x, 9 : rows + 9]
            prod[at + x, 2 * rows : 3 * rows] = here * ext[at + x, 10 : rows + 10]
            base = ext[at + x, 0:8]
            one = base * ext[at + x, 1:9]
            two = base * ext[at + x, 2:10]
            prod[at + x, 3 * rows : 3 * rows + 8] = jnp.where(low_tile >= 6, two, pltpu.roll(one, 6, 0))
            return carry

        lax.fori_loop(0, cells, product, 0, unroll=2)

    copies[3].wait()
    count = lags.shape[0]

    def total(x, carry):
        low, high = edges(x, mate_twin, mate_edge)
        mext[x, 6:8] = low
        mext[x, rows + 8 : rows + 10] = high
        acc = None
        for h in range(count):
            term = weights[h] * prod[x + lags[h]]
            acc = term if acc is None else acc + term
        mix[0, 8 : rows + 8] = acc[rows : 2 * rows]
        mix[1, 8 : rows + 8] = acc[2 * rows : 3 * rows]
        extra = acc[3 * rows : 3 * rows + 8]
        mix[0, 0:8] = pltpu.roll(extra, 2, 0)
        mix[1, 0:8] = extra
        done[x] = (
            0.375 * (acc[0:rows] * mext[x, 8 : rows + 8])
            + 0.25 * (acc[rows : 2 * rows] * mext[x, 9 : rows + 9] + mix[0, 7 : rows + 7] * mext[x, 7 : rows + 7])
            + 0.0625 * (acc[2 * rows : 3 * rows] * mext[x, 10 : rows + 10] + mix[1, 6 : rows + 6] * mext[x, 6 : rows + 6])
        )
        return carry

    lax.fori_loop(0, cells, total, 0)
    out[...] = done[...]


def image(place, lags, weights, own, near, far, halos, mate, mate_halos):
    cells, rows, depth = own.shape
    smem = pl.BlockSpec(memory_space=pltpu.SMEM)
    vmem = pl.BlockSpec(memory_space=pltpu.VMEM)
    hbm = pl.BlockSpec(memory_space=pl.ANY)
    user = jnp.zeros((1,), jnp.int32)
    return pl.pallas_call(
        image_kernel,
        out_shape=jax.ShapeDtypeStruct((cells, rows, depth), F32),
        in_specs=[smem] * 4 + [hbm] * 3 + [vmem] * 6 + [hbm] + [vmem] * 2,
        out_specs=vmem,
        scratch_shapes=[
            pltpu.VMEM((3 * cells, rows + 16, depth), F32),
            pltpu.VMEM((3 * cells, 3 * rows + 8, depth), F32),
            pltpu.VMEM((2, rows + 8, depth), F32),
            pltpu.VMEM((cells, rows + 16, depth), F32),
            pltpu.VMEM((cells, rows, depth), F32),
            pltpu.SemaphoreType.DMA((4,)),
        ],
        compiler_params=pltpu.CompilerParams(vmem_limit_bytes=40 * 2**20),
        cost_estimate=pl.CostEstimate(flops=22 * 10**6, bytes_accessed=4 * 10**6, transcendentals=0),
    )(place, lags, weights, user, own, near, far, *halos, mate, *mate_halos)


def local(routes, source_snaps, receiver_snaps, snap_pairs, offset_lags, weight_table, weight_index):
    pairs = snap_pairs.shape[0]
    cells = source_snaps.shape[1]
    rows = source_snaps.shape[2]
    send = lambda value, route: lax.ppermute(value, ("gx", "gy"), routes[route])
    odd = lax.axis_index("gx") % 2
    second = lax.axis_index("gy") % 2
    place = jnp.stack([odd, second]).astype(jnp.int32)

    fields = []
    for p in range(pairs):
        fields.append(receiver_snaps[snap_pairs[p, 1]])
        fields.append(source_snaps[snap_pairs[p, 0]])
    n = len(fields)

    def toward(block, near_twin):
        low, high = block[:, :2], block[:, rows - 2 :]
        return jnp.where((second == 0) == near_twin, high, low)

    own_twin = send(jnp.stack([toward(f, True) for f in fields]), "twins")
    own_edge = send(jnp.stack([toward(f, False) for f in fields]), "seam")
    near_edge = send(own_edge, "across_edge")
    far_edge = send(near_edge, "onward_edge")

    near, far, near_twin, far_twin = [], [], [], []
    for f in fields:
        near.append(send(f, "across"))
        far.append(send(near[-1], "onward"))
        near_twin.append(send(toward(near[-1], True), "twins"))
        far_twin.append(send(toward(far[-1], True), "twins"))

    outs = []
    for u in range(n):
        p, mate = u // 2, u ^ 1
        sign = 2 if u % 2 == 0 else -2
        outs.append(
            image(
                place,
                cells + sign * offset_lags,
                weight_table[weight_index[p]],
                fields[u],
                near[u],
                far[u],
                (own_twin[u], own_edge[u], near_twin[u], near_edge[u], far_twin[u], far_edge[u]),
                fields[mate],
                (own_twin[mate], own_edge[mate]),
            )
        )
    return jnp.stack(outs[0::2]), jnp.stack(outs[1::2])


def solution(mesh):
    routes = moves(mesh)
    split = P(None, "gx", "gy", None)
    return jax.shard_map(
        functools.partial(local, routes),
        mesh=mesh,
        in_specs=(split, split, P(), P(), P(), P()),
        out_specs=(split, split),
        check_vma=False,
    )
```

```python
import functools

import jax
import jax.numpy as jnp
from jax import lax
from jax.experimental import pallas as pl
from jax.experimental.pallas import tpu as pltpu
from jax.sharding import PartitionSpec as P

F32 = jnp.float32
SMEM = pl.BlockSpec(memory_space=pltpu.SMEM)
VMEM = pl.BlockSpec(memory_space=pltpu.VMEM)
HBM = pl.BlockSpec(memory_space=pl.ANY)

ODD, SECOND, COUNT, FIELD, SLOT, FIRST, ORDER, LAG = 0, 1, 2, 8, 16, 24, 32, 40


def moves(mesh):
    nx, ny = mesh.shape["gx"], mesh.shape["gy"]
    flat = lambda x, y: x * ny + y
    middle = list(range(1, ny - 1))
    across = [(x, x ^ 1) for x in range(nx) if x ^ 1 < nx]
    onward = [(x, x + 2) for x in range(0, nx - 2, 2)] + [(x, x - 2) for x in range(3, nx, 2)]
    whole = lambda route, rows: [(flat(a, y), flat(b, y)) for a, b in route for y in rows]
    seams = [(a, b) for y in range(1, ny - 1, 2) for a, b in ((y, y + 1), (y + 1, y))]
    return {
        "across": whole(across, range(ny)),
        "onward": whole(onward, range(ny)),
        "across_edge": whole(across, middle),
        "onward_edge": whole(onward, middle),
        "twins": [(flat(x, y), flat(x, y ^ 1)) for x in range(nx) for y in range(ny)],
        "seam": [(flat(x, a), flat(x, b)) for x in range(nx) for a, b in seams],
    }


def plan_kernel(snaps, pairs, lags, table, rows, plan, weights):
    units = 2 * pairs.shape[0]
    plan[ODD] = lax.rem(lax.axis_index("gx"), 2)
    plan[SECOND] = lax.rem(lax.axis_index("gy"), 2)
    ids = [pairs[u // 2, 1] if u % 2 == 0 else pairs[u // 2, 0] + snaps for u in range(units)]
    same = [[(ids[u] == ids[v]).astype(jnp.int32) for v in range(units)] for u in range(units)]
    uses = [sum(same[u]) for u in range(units)]
    leads = [jnp.int32(1)]
    for u in range(1, units):
        leads.append((sum(same[u][:u]) == 0).astype(jnp.int32))
    rank = []
    for u in range(units):
        ahead = jnp.int32(0)
        for v in range(units):
            if v != u:
                sooner = uses[v] >= uses[u] if v < u else uses[v] > uses[u]
                ahead = ahead + leads[v] * sooner.astype(jnp.int32)
        rank.append(ahead)
    slots = [sum(same[u][v] * leads[v] * rank[v] for v in range(units)) for u in range(units)]
    plan[COUNT] = sum(leads)
    for u in range(units):
        plan[SLOT + u] = slots[u]
        plan[FIELD + slots[u]] = ids[u]
        before = jnp.int32(0)
        for v in range(units):
            if v != u:
                sooner = slots[v] <= slots[u] if v < u else slots[v] < slots[u]
                before = before + sooner.astype(jnp.int32)
        plan[ORDER + before] = u
        plan[FIRST + u] = sum((slots[v] < u).astype(jnp.int32) for v in range(units))
    plan[FIRST + units] = units
    for h in range(lags.shape[0]):
        plan[LAG + h] = 2 * lags[h]
        for p in range(pairs.shape[0]):
            weights[p * lags.shape[0] + h] = table[rows[p], h]


def fetch(plan, slot_field, source, receiver, target, sem):
    snaps = receiver.shape[0]

    @pl.when(slot_field < snaps)
    def _():
        pltpu.make_async_copy(receiver.at[jnp.minimum(slot_field, snaps - 1)], target, sem).start()

    @pl.when(slot_field >= snaps)
    def _():
        pltpu.make_async_copy(source.at[jnp.maximum(slot_field - snaps, 0)], target, sem).start()

    return pltpu.make_async_copy(receiver.at[0], target, sem)


def take_kernel(slot, plan, source, receiver, *rest):
    out, sem = rest[-2:]
    fetch(plan, plan[FIELD + slot], source, receiver, out, sem).wait()


def take(slot, plan, source, receiver, *earlier):
    return pl.pallas_call(
        functools.partial(take_kernel, slot),
        out_shape=jax.ShapeDtypeStruct(source.shape[1:], F32),
        in_specs=[SMEM] + [HBM] * (2 + len(earlier)),
        out_specs=HBM,
        scratch_shapes=[pltpu.SemaphoreType.DMA],
        cost_estimate=pl.CostEstimate(flops=0, bytes_accessed=1600000, transcendentals=0),
    )(plan, source, receiver, *earlier)


def cut_kernel(passed, plan, block, *rest):
    inner, tile, sem = rest[-3:]
    cells, rows, _ = block.shape
    second = plan[SECOND]
    copy = pltpu.make_async_copy(block.at[:, pl.ds(pl.multiple_of((1 - second) * (rows - 8), 8), 8)], tile, sem)
    copy.start()
    copy.wait()

    def cut(x, carry):
        inner[x] = jnp.where(second == 1, tile[x, 0:2], tile[x, 6:8])
        return carry

    lax.fori_loop(0, cells, cut, 0, unroll=4)


def cut(plan, block, *earlier, passed=False):
    cells, _, depth = block.shape
    edge = jax.ShapeDtypeStruct((cells, 2, depth), F32)
    return pl.pallas_call(
        functools.partial(cut_kernel, passed),
        out_shape=[jax.ShapeDtypeStruct(block.shape, F32), edge] if passed else edge,
        in_specs=[SMEM] + [HBM] * (1 + len(earlier)),
        out_specs=[HBM, VMEM] if passed else VMEM,
        input_output_aliases={1: 0} if passed else {},
        scratch_shapes=[pltpu.VMEM((cells, 8, depth), F32), pltpu.SemaphoreType.DMA],
        cost_estimate=pl.CostEstimate(flops=0, bytes_accessed=1000000, transcendentals=0),
    )(plan, block, *earlier)


def rim_kernel(count, plan, source, receiver, inner, outer, low, high, sems):
    snaps, cells, rows, _ = receiver.shape
    waits = []
    for s in range(count):
        field = plan[FIELD + s]
        for side, (target, at) in enumerate(((low, 0), (high, rows - 8))):
            sem = sems.at[side, s]

            @pl.when(field < snaps)
            def _():
                block = receiver.at[jnp.minimum(field, snaps - 1)]
                pltpu.make_async_copy(block.at[:, pl.ds(at, 8)], target.at[s], sem).start()

            @pl.when(field >= snaps)
            def _():
                block = source.at[jnp.maximum(field - snaps, 0)]
                pltpu.make_async_copy(block.at[:, pl.ds(at, 8)], target.at[s], sem).start()

            waits.append(pltpu.make_async_copy(receiver.at[0, :, pl.ds(at, 8)], target.at[s], sem))
    for wait in waits:
        wait.wait()
    second = plan[SECOND] == 1

    for s in range(count):

        def cut(x, carry):
            a, b = low[s, x, 0:2], high[s, x, 6:8]
            inner[s, x] = jnp.where(second, a, b)
            outer[s, x] = jnp.where(second, b, a)
            return carry

        lax.fori_loop(0, cells, cut, 0, unroll=4)


def rim(plan, source, receiver, count):
    _, cells, rows, depth = source.shape
    edge = jax.ShapeDtypeStruct((count, cells, 2, depth), F32)
    return pl.pallas_call(
        functools.partial(rim_kernel, count),
        out_shape=[edge, edge],
        in_specs=[SMEM, HBM, HBM],
        out_specs=[VMEM, VMEM],
        scratch_shapes=[
            pltpu.VMEM((count, cells, 8, depth), F32),
            pltpu.VMEM((count, cells, 8, depth), F32),
            pltpu.SemaphoreType.DMA((2, count)),
        ],
        cost_estimate=pl.CostEstimate(flops=0, bytes_accessed=6000000, transcendentals=0),
    )(plan, source, receiver)


def image_kernel(slot, plan, weights, source, receiver, near, far, own_twin, own_edge, near_twin, near_edge, far_twin, far_edge, *rest):
    to_source, to_receiver, token, ext, prod, mix, mext, done, sems = rest[-9:]
    _, cells, rows, _ = source.shape
    taps = weights.shape[0] // to_source.shape[0]
    odd, second = plan[ODD], plan[SECOND] == 1
    near_at = jnp.where(odd == 1, 0, 2 * cells)
    far_at = 2 * cells - near_at

    def inside(target, at):
        return target.at[pl.ds(at, cells), pl.ds(8, rows)]

    waits = [
        fetch(plan, plan[FIELD + slot], source, receiver, inside(ext, cells), sems.at[0]),
        pltpu.make_async_copy(near, inside(ext, near_at), sems.at[1]),
        pltpu.make_async_copy(far, inside(ext, far_at), sems.at[2]),
    ]
    waits[1].start()
    waits[2].start()
    low_tile = lax.broadcasted_iota(jnp.int32, (8, ext.shape[2]), 0)

    def border(target, at, twin, edge):
        target[at, 6:8] = jnp.where(second, twin, edge)
        target[at, rows + 8 : rows + 10] = jnp.where(second, edge, twin)

    spots = (
        (cells, lambda x: own_twin[slot, x], lambda x: own_edge[slot, x]),
        (near_at, lambda x: near_twin[x], lambda x: near_edge[slot, x]),
        (far_at, lambda x: far_twin[x], lambda x: far_edge[slot, x]),
    )
    for wait, (at, twin, edge) in zip(waits, spots):
        wait.wait()

        def product(x, carry):
            border(ext, at + x, twin(x), edge(x))
            here = ext[at + x, 8 : rows + 8]
            prod[at + x, 0:rows] = here * here
            prod[at + x, rows : 2 * rows] = here * ext[at + x, 9 : rows + 9]
            prod[at + x, 2 * rows : 3 * rows] = here * ext[at + x, 10 : rows + 10]
            base = ext[at + x, 0:8]
            one = base * ext[at + x, 1:9]
            two = base * ext[at + x, 2:10]
            prod[at + x, 3 * rows : 3 * rows + 8] = jnp.where(low_tile >= 6, two, pltpu.roll(one, 6, 0))
            return carry

        lax.fori_loop(0, cells, product, 0, unroll=2)

    def unit(index, carry):
        u = plan[ORDER + index]
        to_r = lax.rem(u, 2)
        p = lax.div(u, 2)
        mate_slot = plan[SLOT + u + 1 - 2 * to_r]
        fetch(plan, plan[FIELD + mate_slot], source, receiver, inside(mext, 0), sems.at[3]).wait()
        sign = 1 - 2 * to_r
        at = [cells + sign * plan[LAG + h] for h in range(taps)]
        scale = [weights[p * taps + h] for h in range(taps)]

        def total(x, carry):
            border(mext, x, own_twin[mate_slot, x], own_edge[mate_slot, x])
            acc = None
            for h in range(taps):
                term = scale[h] * prod[x + at[h]]
                acc = term if acc is None else acc + term
            mix[0, 8 : rows + 8] = acc[rows : 2 * rows]
            mix[1, 8 : rows + 8] = acc[2 * rows : 3 * rows]
            extra = acc[3 * rows : 3 * rows + 8]
            mix[0, 0:8] = pltpu.roll(extra, 2, 0)
            mix[1, 0:8] = extra
            one = acc[rows : 2 * rows] * mext[x, 9 : rows + 9] + mix[0, 7 : rows + 7] * mext[x, 7 : rows + 7]
            two = acc[2 * rows : 3 * rows] * mext[x, 10 : rows + 10] + mix[1, 6 : rows + 6] * mext[x, 6 : rows + 6]
            done[x] = 0.375 * (acc[0:rows] * mext[x, 8 : rows + 8]) + 0.25 * one + 0.0625 * two
            return carry

        lax.fori_loop(0, cells, total, 0)
        for which, target in enumerate((to_source, to_receiver)):

            @pl.when(to_r == which)
            def _():
                out = pltpu.make_async_copy(done, target.at[p], sems.at[4])
                out.start()
                out.wait()

        return carry

    lax.fori_loop(plan[FIRST + slot], plan[FIRST + slot + 1], unit, 0)
    token[...] = jnp.zeros_like(token)


def image(slot, pairs, plan, weights, source, receiver, near, far, halos, outs):
    _, cells, rows, depth = source.shape
    whole = jax.ShapeDtypeStruct((pairs, cells, rows, depth), F32)
    return pl.pallas_call(
        functools.partial(image_kernel, slot),
        out_shape=[whole, whole, jax.ShapeDtypeStruct((8, 128), F32)],
        in_specs=[SMEM] * 2 + [HBM] * 4 + [VMEM] * 6 + [HBM] * len(outs),
        out_specs=[HBM, HBM, VMEM],
        input_output_aliases={12 + i: i for i in range(len(outs))},
        scratch_shapes=[
            pltpu.VMEM((3 * cells, rows + 16, depth), F32),
            pltpu.VMEM((3 * cells, 3 * rows + 8, depth), F32),
            pltpu.VMEM((2, rows + 8, depth), F32),
            pltpu.VMEM((cells, rows + 16, depth), F32),
            pltpu.VMEM((cells, rows, depth), F32),
            pltpu.SemaphoreType.DMA((5,)),
        ],
        compiler_params=pltpu.CompilerParams(vmem_limit_bytes=58 * 2**20),
        cost_estimate=pl.CostEstimate(flops=22 * 10**6, bytes_accessed=12 * 10**6, transcendentals=0),
    )(plan, weights, source, receiver, near, far, *halos, *outs)


def work(count, pairs, routes, plan, weights, source, receiver):
    send = lambda value, route: lax.ppermute(value, ("gx", "gy"), routes[route])

    near = [send(take(0, plan, source, receiver), "across")]
    inner, outer = rim(plan, source, receiver, count)
    own_twin = send(inner, "twins")
    own_edge = send(outer, "seam")
    near.append(send(take(1, plan, source, receiver), "across"))
    near_edge = send(own_edge, "across_edge")
    far_edge = send(near_edge, "onward_edge")

    far, near_twin, far_twin, tokens = [], [], [], []
    outs = ()

    def step(s):
        earlier = tokens[s - 2 : s - 1] if s >= 2 else []
        if s == 2:
            earlier = earlier + [far_edge]
        near[s], facing = cut(plan, near[s], *earlier, passed=True)
        far.append(send(near[s], "onward"))
        near_twin.append(send(facing, "twins"))

    for s in range(count):
        if s >= 2:
            earlier = [near[s - 2], near_twin[s - 2]]
            if s == 2:
                earlier += [own_twin, own_edge]
            if s == 3:
                earlier += [near_edge]
            if s >= 3:
                earlier += [far[s - 3], far_twin[s - 3]]
            near.append(send(take(s, plan, source, receiver, *earlier), "across"))
        step(s)
        far_twin.append(send(cut(plan, far[s]), "twins"))
        halos = (own_twin, own_edge, near_twin[s], near_edge, far_twin[s], far_edge)
        *outs, token = image(s, pairs, plan, weights, source, receiver, near[s], far[s], halos, outs)
        tokens.append(token)
    return tuple(outs)


def local(routes, source_snaps, receiver_snaps, snap_pairs, offset_lags, weight_table, weight_index):
    pairs = snap_pairs.shape[0]
    plan, weights = pl.pallas_call(
        functools.partial(plan_kernel, receiver_snaps.shape[0]),
        out_shape=[
            jax.ShapeDtypeStruct((LAG + offset_lags.shape[0],), jnp.int32),
            jax.ShapeDtypeStruct((pairs * offset_lags.shape[0],), F32),
        ],
        in_specs=[SMEM] * 4,
        out_specs=[SMEM] * 2,
    )(snap_pairs, offset_lags, weight_table, weight_index)
    least = 2
    most = 2 * pairs
    branches = [functools.partial(work, count, pairs, routes) for count in range(least, most + 1)]
    return lax.switch(plan[COUNT] - least, branches, plan, weights, source_snaps, receiver_snaps)


def solution(mesh):
    routes = moves(mesh)
    split = P(None, "gx", "gy", None)
    return jax.shard_map(
        functools.partial(local, routes),
        mesh=mesh,
        in_specs=(split, split, P(), P(), P(), P()),
        out_specs=(split, split),
        check_vma=False,
    )
```

```python
import functools

import jax
import jax.numpy as jnp
from jax import lax
from jax.experimental import pallas as pl
from jax.experimental.pallas import tpu as pltpu
from jax.sharding import PartitionSpec as P

F32 = jnp.float32
SMEM = pl.BlockSpec(memory_space=pltpu.SMEM)
VMEM = pl.BlockSpec(memory_space=pltpu.VMEM)
HBM = pl.BlockSpec(memory_space=pl.ANY)
MAIN = pl.BlockSpec(memory_space=pltpu.HBM)
SCOPED = 24 * 2**20

ODD, SECOND, COUNT, FIELD, SLOT, FIRST, ORDER, LAG = 0, 1, 2, 8, 16, 24, 32, 40


def moves(mesh):
    nx, ny = mesh.shape["gx"], mesh.shape["gy"]
    flat = lambda x, y: x * ny + y
    middle = list(range(1, ny - 1))
    across = [(x, x ^ 1) for x in range(nx) if x ^ 1 < nx]
    onward = [(x, x + 2) for x in range(0, nx - 2, 2)] + [(x, x - 2) for x in range(3, nx, 2)]
    whole = lambda route, rows: [(flat(a, y), flat(b, y)) for a, b in route for y in rows]
    seams = [(a, b) for y in range(1, ny - 1, 2) for a, b in ((y, y + 1), (y + 1, y))]
    return {
        "across": whole(across, range(ny)),
        "onward": whole(onward, range(ny)),
        "across_edge": whole(across, middle),
        "onward_edge": whole(onward, middle),
        "twins": [(flat(x, y), flat(x, y ^ 1)) for x in range(nx) for y in range(ny)],
        "seam": [(flat(x, a), flat(x, b)) for x in range(nx) for a, b in seams],
    }


def plan_kernel(snaps, pairs, lags, table, rows, plan, weights):
    units = 2 * pairs.shape[0]
    plan[ODD] = lax.rem(lax.axis_index("gx"), 2)
    plan[SECOND] = lax.rem(lax.axis_index("gy"), 2)
    ids = [pairs[u // 2, 1] if u % 2 == 0 else pairs[u // 2, 0] + snaps for u in range(units)]
    same = [[(ids[u] == ids[v]).astype(jnp.int32) for v in range(units)] for u in range(units)]
    uses = [sum(same[u]) for u in range(units)]
    leads = [jnp.int32(1)]
    for u in range(1, units):
        leads.append((sum(same[u][:u]) == 0).astype(jnp.int32))
    rank = []
    for u in range(units):
        ahead = jnp.int32(0)
        for v in range(units):
            if v != u:
                sooner = uses[v] >= uses[u] if v < u else uses[v] > uses[u]
                ahead = ahead + leads[v] * sooner.astype(jnp.int32)
        rank.append(ahead)
    slots = [sum(same[u][v] * leads[v] * rank[v] for v in range(units)) for u in range(units)]
    plan[COUNT] = sum(leads)
    for u in range(units):
        plan[SLOT + u] = slots[u]
        plan[FIELD + slots[u]] = ids[u]
        before = jnp.int32(0)
        for v in range(units):
            if v != u:
                sooner = slots[v] <= slots[u] if v < u else slots[v] < slots[u]
                before = before + sooner.astype(jnp.int32)
        plan[ORDER + before] = u
        plan[FIRST + u] = sum((slots[v] < u).astype(jnp.int32) for v in range(units))
    plan[FIRST + units] = units
    for h in range(lags.shape[0]):
        plan[LAG + h] = 2 * lags[h]
        for p in range(pairs.shape[0]):
            weights[p * lags.shape[0] + h] = table[rows[p], h]


def fetch(field, source, receiver, target, sem):
    snaps = receiver.shape[0]

    @pl.when(field < snaps)
    def _():
        pltpu.make_async_copy(receiver.at[jnp.minimum(field, snaps - 1)], target, sem).start()

    @pl.when(field >= snaps)
    def _():
        pltpu.make_async_copy(source.at[jnp.maximum(field - snaps, 0)], target, sem).start()

    return pltpu.make_async_copy(receiver.at[0], target, sem)


def lead_kernel(plan, source, receiver, out, sem):
    fetch(plan[FIELD], source, receiver, out, sem).wait()


def lead(plan, source, receiver):
    return pl.pallas_call(
        lead_kernel,
        out_shape=jax.ShapeDtypeStruct(source.shape[1:], F32),
        in_specs=[SMEM, HBM, HBM],
        out_specs=VMEM,
        scratch_shapes=[pltpu.SemaphoreType.DMA],
        compiler_params=pltpu.CompilerParams(vmem_limit_bytes=SCOPED),
        cost_estimate=pl.CostEstimate(flops=0, bytes_accessed=1600000, transcendentals=0),
    )(plan, source, receiver)


def gather_kernel(plan, source, receiver, fields, inner, outer, sems):
    count, cells, rows, _ = fields.shape
    waits = [fetch(plan[FIELD + s], source, receiver, fields.at[s], sems.at[s]) for s in range(count)]
    second = plan[SECOND] == 1
    for s, wait in enumerate(waits):
        wait.wait()

        def rim(x, carry):
            low, high = fields[s, x, 0:2], fields[s, x, rows - 2 : rows]
            inner[s, x] = jnp.where(second, low, high)
            outer[s, x] = jnp.where(second, high, low)
            return carry

        lax.fori_loop(0, cells, rim, 0, unroll=4)


def gather(plan, source, receiver, count):
    _, cells, rows, depth = source.shape
    edge = jax.ShapeDtypeStruct((count, cells, 2, depth), F32)
    return pl.pallas_call(
        gather_kernel,
        out_shape=[jax.ShapeDtypeStruct((count, cells, rows, depth), F32), edge, edge],
        in_specs=[SMEM, HBM, HBM],
        out_specs=[VMEM] * 3,
        scratch_shapes=[pltpu.SemaphoreType.DMA((count,))],
        compiler_params=pltpu.CompilerParams(vmem_limit_bytes=SCOPED),
        cost_estimate=pl.CostEstimate(flops=0, bytes_accessed=6000000, transcendentals=0),
    )(plan, source, receiver)


def take_kernel(slot, fields, *rest):
    out, sem = rest[-2:]
    copy = pltpu.make_async_copy(fields.at[slot], out, sem)
    copy.start()
    copy.wait()


def take(slot, fields, *earlier):
    return pl.pallas_call(
        functools.partial(take_kernel, slot),
        out_shape=jax.ShapeDtypeStruct(fields.shape[1:], F32),
        in_specs=[HBM] * (1 + len(earlier)),
        out_specs=VMEM,
        scratch_shapes=[pltpu.SemaphoreType.DMA],
        compiler_params=pltpu.CompilerParams(vmem_limit_bytes=SCOPED),
        cost_estimate=pl.CostEstimate(flops=0, bytes_accessed=1600000, transcendentals=0),
    )(fields, *earlier)


def cut_kernel(many, plan, *rest):
    blocks, inner = rest[:many], rest[-1]
    cells, rows, _ = blocks[0].shape
    second = plan[SECOND] == 1
    for i, block in enumerate(blocks):

        def rim(x, carry):
            inner[i, x] = jnp.where(second, block[x, 0:2], block[x, rows - 2 : rows])
            return carry

        lax.fori_loop(0, cells, rim, 0, unroll=4)


def cut(plan, blocks, earlier):
    cells, _, depth = blocks[0].shape
    return pl.pallas_call(
        functools.partial(cut_kernel, len(blocks)),
        out_shape=jax.ShapeDtypeStruct((len(blocks), cells, 2, depth), F32),
        in_specs=[SMEM] + [VMEM] * len(blocks) + [HBM] * len(earlier),
        out_specs=VMEM,
        compiler_params=pltpu.CompilerParams(vmem_limit_bytes=SCOPED),
        cost_estimate=pl.CostEstimate(flops=0, bytes_accessed=1000000, transcendentals=0),
    )(plan, *blocks, *earlier)


def image_kernel(
    slot, spot, plan, weights, fields, near, far, own_twin, own_edge, near_twin, near_edge, far_twin, far_edge, *rest
):
    to_source, to_receiver, token, ext, prod, mix, mext, done, sems = rest[-9:]
    _, cells, rows, depth = fields.shape
    halves = ext.shape[0]
    lanes = depth // halves
    pairs = to_source.shape[0]
    taps = weights.shape[0] // pairs
    odd, second = plan[ODD], plan[SECOND] == 1
    near_at = jnp.where(odd == 1, 0, 2 * cells)
    far_at = 2 * cells - near_at
    first, last = plan[FIRST + slot], plan[FIRST + slot + 1]
    part = [slice(z * lanes, (z + 1) * lanes) for z in range(halves)]
    low_tile = lax.broadcasted_iota(jnp.int32, (8, lanes), 0)

    def widen(target, at, block, twin, edge):
        def one(x, carry):
            for z in range(halves):
                t, e = twin[x, :, part[z]], edge[x, :, part[z]]
                target[z, at + x, 8 : rows + 8] = block[x, :, part[z]]
                target[z, at + x, 6:8] = jnp.where(second, t, e)
                target[z, at + x, rows + 8 : rows + 10] = jnp.where(second, e, t)
            return carry

        lax.fori_loop(0, cells, one, 0, unroll=4)

    widen(ext, cells, fields.at[slot], own_twin.at[slot], own_edge.at[slot])
    widen(ext, near_at, near, near_twin.at[0], near_edge.at[slot])
    widen(ext, far_at, far, far_twin.at[spot], far_edge.at[slot])

    def product(x, carry):
        for z in range(halves):
            e, q = ext.at[z, x], prod.at[z, x]
            here = e[8 : rows + 8]
            q[0:rows] = here * here
            q[rows : 2 * rows] = here * e[9 : rows + 9]
            q[2 * rows : 3 * rows] = here * e[10 : rows + 10]
            base = e[0:8]
            one = base * e[1:9]
            two = base * e[2:10]
            q[3 * rows : 3 * rows + 8] = jnp.where(low_tile >= 6, two, pltpu.roll(one, 6, 0))
        return carry

    lax.fori_loop(0, 3 * cells, product, 0, unroll=4)

    def unit(index, carry):
        i = index - first
        u = plan[ORDER + index]
        to_r = lax.rem(u, 2)
        p = lax.div(u, 2)
        mate = plan[SLOT + u + 1 - 2 * to_r]
        sign = 1 - 2 * to_r
        at = [cells + sign * plan[LAG + h] for h in range(taps)]
        scale = [weights[p * taps + h] for h in range(taps)]
        widen(mext, 0, fields.at[mate], own_twin.at[mate], own_edge.at[mate])

        def total(x, carry):
            for z in range(halves):
                m, s = mix.at[z], mext.at[z, x]
                acc = None
                for h in range(taps):
                    term = scale[h] * prod[z, x + at[h]]
                    acc = term if acc is None else acc + term
                m[0, 8 : rows + 8] = acc[rows : 2 * rows]
                m[1, 8 : rows + 8] = acc[2 * rows : 3 * rows]
                extra = acc[3 * rows : 3 * rows + 8]
                m[0, 0:8] = pltpu.roll(extra, 2, 0)
                m[1, 0:8] = extra
                one = acc[rows : 2 * rows] * s[9 : rows + 9] + m[0, 7 : rows + 7] * s[7 : rows + 7]
                two = acc[2 * rows : 3 * rows] * s[10 : rows + 10] + m[1, 6 : rows + 6] * s[6 : rows + 6]
                done[i, x, :, part[z]] = 0.375 * (acc[0:rows] * s[8 : rows + 8]) + 0.25 * one + 0.0625 * two
            return carry

        lax.fori_loop(0, cells, total, 0)
        for which, target in enumerate((to_source, to_receiver)):

            @pl.when(to_r == which)
            def _():
                pltpu.make_async_copy(done.at[i], target.at[p], sems.at[i]).start()

        return carry

    lax.fori_loop(first, last, unit, 0)

    def settle(index, carry):
        i = index - first
        pltpu.make_async_copy(done.at[i], to_source.at[0], sems.at[i]).wait()
        return carry

    lax.fori_loop(first, last, settle, 0)
    token[...] = jnp.zeros_like(token)


def image(slot, pairs, plan, weights, fields, near, far, halos, spot, outs):
    _, cells, rows, depth = fields.shape
    whole = jax.ShapeDtypeStruct((pairs, cells, rows, depth), F32)
    halves = 2
    lanes = depth // halves
    return pl.pallas_call(
        functools.partial(image_kernel, slot, spot),
        out_shape=[whole, whole, jax.ShapeDtypeStruct((8, 128), F32)],
        in_specs=[SMEM] * 2 + [VMEM] * 9 + [MAIN] * len(outs),
        out_specs=[MAIN, MAIN, VMEM],
        input_output_aliases={11 + i: i for i in range(len(outs))},
        scratch_shapes=[
            pltpu.VMEM((halves, 3 * cells, rows + 16, lanes), F32),
            pltpu.VMEM((halves, 3 * cells, 3 * rows + 8, lanes), F32),
            pltpu.VMEM((halves, 2, rows + 8, lanes), F32),
            pltpu.VMEM((halves, cells, rows + 16, lanes), F32),
            pltpu.VMEM((pairs, cells, rows, depth), F32),
            pltpu.SemaphoreType.DMA((pairs,)),
        ],
        compiler_params=pltpu.CompilerParams(vmem_limit_bytes=SCOPED),
        cost_estimate=pl.CostEstimate(flops=22 * 10**6, bytes_accessed=22 * 10**6, transcendentals=0),
    )(plan, weights, fields, near, far, *halos, *outs)


def work(count, pairs, routes, plan, weights, source, receiver):
    send = lambda value, route: lax.ppermute(value, ("gx", "gy"), routes[route])

    near = [send(lead(plan, source, receiver), "across")]
    fields, inner, outer = gather(plan, source, receiver, count)
    own_twin = send(inner, "twins")
    own_edge = send(outer, "seam")
    near.append(send(take(1, fields), "across"))
    near_edge = send(own_edge, "across_edge")
    far_edge = send(near_edge, "onward_edge")

    far, twins, tokens = [], [], []
    outs = ()
    for s in range(count + 1):
        if s < count:
            far.append(send(near[s], "onward"))
            if s + 2 < count:
                earlier = [near[s], own_twin, own_edge] if s == 0 else [near[s], far[s - 1], near_edge, twins[s - 1]]
                earlier = earlier + tokens[s - 2 : s - 1] if s >= 2 else earlier
                near.append(send(take(s + 2, fields, *earlier), "across"))
        blocks = near[s : s + 1] + (far[s - 1 : s] if s >= 1 else [])
        twins.append(send(cut(plan, blocks, tokens[s - 2 : s - 1] if s >= 2 else []), "twins"))
        if s >= 1:
            halos = (own_twin, own_edge, twins[s - 1], near_edge, twins[s], far_edge)
            *outs, token = image(s - 1, pairs, plan, weights, fields, near[s - 1], far[s - 1], halos, len(blocks) - 1, outs)
            tokens.append(token)
    return tuple(outs)


def local(routes, source_snaps, receiver_snaps, snap_pairs, offset_lags, weight_table, weight_index):
    pairs = snap_pairs.shape[0]
    plan, weights = pl.pallas_call(
        functools.partial(plan_kernel, receiver_snaps.shape[0]),
        out_shape=[
            jax.ShapeDtypeStruct((LAG + offset_lags.shape[0],), jnp.int32),
            jax.ShapeDtypeStruct((pairs * offset_lags.shape[0],), F32),
        ],
        in_specs=[SMEM] * 4,
        out_specs=[SMEM] * 2,
    )(snap_pairs, offset_lags, weight_table, weight_index)
    least = 2
    most = 2 * pairs
    branches = [functools.partial(work, count, pairs, routes) for count in range(least, most + 1)]
    return lax.switch(plan[COUNT] - least, branches, plan, weights, source_snaps, receiver_snaps)


def solution(mesh):
    routes = moves(mesh)
    split = P(None, "gx", "gy", None)
    return jax.shard_map(
        functools.partial(local, routes),
        mesh=mesh,
        in_specs=(split, split, P(), P(), P(), P()),
        out_specs=(split, split),
        check_vma=False,
    )
```

```python
import functools

import jax
import jax.numpy as jnp
from jax import lax
from jax.experimental import pallas as pl
from jax.experimental.pallas import tpu as pltpu
from jax.sharding import PartitionSpec as P

F32 = jnp.float32
SMEM = pl.BlockSpec(memory_space=pltpu.SMEM)
VMEM = pl.BlockSpec(memory_space=pltpu.VMEM)
HBM = pl.BlockSpec(memory_space=pl.ANY)
MAIN = pl.BlockSpec(memory_space=pltpu.HBM)
SCOPED = 24 * 2**20

ODD, SECOND, COUNT, FIELD, SLOT, FIRST, ORDER, LAG = 0, 1, 2, 8, 16, 24, 32, 40


def moves(mesh):
    nx, ny = mesh.shape["gx"], mesh.shape["gy"]
    flat = lambda x, y: x * ny + y
    across = [(x, x ^ 1) for x in range(nx) if x ^ 1 < nx]
    onward = [(x, x + 2) for x in range(0, nx - 2, 2)] + [(x, x - 2) for x in range(3, nx, 2)]
    whole = lambda route, rows: [(flat(a, y), flat(b, y)) for a, b in route for y in rows]
    seams = [(a, b) for y in range(1, ny - 1, 2) for a, b in ((y, y + 1), (y + 1, y))]
    return {
        "across": whole(across, range(ny)),
        "onward": whole(onward, range(ny)),
        "twins": [(flat(x, y), flat(x, y ^ 1)) for x in range(nx) for y in range(ny)],
        "seam": [(flat(x, a), flat(x, b)) for x in range(nx) for a, b in seams],
        "seam_near": [(flat(x, a), flat(t, b)) for x, t in across for a, b in seams],
        "seam_far": [(flat(x ^ 1, a), flat(t, b)) for x, t in onward for a, b in seams],
    }


def plan_kernel(snaps, pairs, lags, table, rows, plan, weights):
    units = 2 * pairs.shape[0]
    plan[ODD] = lax.rem(lax.axis_index("gx"), 2)
    plan[SECOND] = lax.rem(lax.axis_index("gy"), 2)
    ids = [pairs[u // 2, 1] if u % 2 == 0 else pairs[u // 2, 0] + snaps for u in range(units)]
    same = [[(ids[u] == ids[v]).astype(jnp.int32) for v in range(units)] for u in range(units)]
    uses = [sum(same[u]) for u in range(units)]
    leads = [jnp.int32(1)]
    for u in range(1, units):
        leads.append((sum(same[u][:u]) == 0).astype(jnp.int32))
    rank = []
    for u in range(units):
        ahead = jnp.int32(0)
        for v in range(units):
            if v != u:
                sooner = uses[v] >= uses[u] if v < u else uses[v] > uses[u]
                ahead = ahead + leads[v] * sooner.astype(jnp.int32)
        rank.append(ahead)
    slots = [sum(same[u][v] * leads[v] * rank[v] for v in range(units)) for u in range(units)]
    plan[COUNT] = sum(leads)
    for u in range(units):
        plan[SLOT + u] = slots[u]
        plan[FIELD + slots[u]] = ids[u]
        before = jnp.int32(0)
        for v in range(units):
            if v != u:
                sooner = slots[v] <= slots[u] if v < u else slots[v] < slots[u]
                before = before + sooner.astype(jnp.int32)
        plan[ORDER + before] = u
        plan[FIRST + u] = sum((slots[v] < u).astype(jnp.int32) for v in range(units))
    plan[FIRST + units] = units
    for h in range(lags.shape[0]):
        plan[LAG + h] = 2 * lags[h]
        for p in range(pairs.shape[0]):
            weights[p * lags.shape[0] + h] = table[rows[p], h]


def fetch(field, source, receiver, target, sem):
    snaps = receiver.shape[0]

    @pl.when(field < snaps)
    def _():
        pltpu.make_async_copy(receiver.at[jnp.minimum(field, snaps - 1)], target, sem).start()

    @pl.when(field >= snaps)
    def _():
        pltpu.make_async_copy(source.at[jnp.maximum(field - snaps, 0)], target, sem).start()

    return pltpu.make_async_copy(receiver.at[0], target, sem)


def lead_kernel(plan, source, receiver, out, sem):
    fetch(plan[FIELD], source, receiver, out, sem).wait()


def lead(plan, source, receiver):
    return pl.pallas_call(
        lead_kernel,
        out_shape=jax.ShapeDtypeStruct(source.shape[1:], F32),
        in_specs=[SMEM, HBM, HBM],
        out_specs=VMEM,
        scratch_shapes=[pltpu.SemaphoreType.DMA],
        compiler_params=pltpu.CompilerParams(vmem_limit_bytes=SCOPED),
        cost_estimate=pl.CostEstimate(flops=0, bytes_accessed=1600000, transcendentals=0),
    )(plan, source, receiver)


def gather_kernel(plan, source, receiver, fields, inner, outer, sems):
    count, cells, rows, _ = fields.shape
    waits = [fetch(plan[FIELD + s], source, receiver, fields.at[s], sems.at[s]) for s in range(count)]
    second = plan[SECOND] == 1
    for s, wait in enumerate(waits):
        wait.wait()

        def rim(x, carry):
            low, high = fields[s, x, 0:2], fields[s, x, rows - 2 : rows]
            inner[s, x] = jnp.where(second, low, high)
            outer[s, x] = jnp.where(second, high, low)
            return carry

        lax.fori_loop(0, cells, rim, 0, unroll=4)


def gather(plan, source, receiver, count):
    _, cells, rows, depth = source.shape
    edge = jax.ShapeDtypeStruct((count, cells, 2, depth), F32)
    return pl.pallas_call(
        gather_kernel,
        out_shape=[jax.ShapeDtypeStruct((count, cells, rows, depth), F32), edge, edge],
        in_specs=[SMEM, HBM, HBM],
        out_specs=[VMEM] * 3,
        scratch_shapes=[pltpu.SemaphoreType.DMA((count,))],
        compiler_params=pltpu.CompilerParams(vmem_limit_bytes=SCOPED),
        cost_estimate=pl.CostEstimate(flops=0, bytes_accessed=6000000, transcendentals=0),
    )(plan, source, receiver)


def take_kernel(slot, fields, *rest):
    out, sem = rest[-2:]
    copy = pltpu.make_async_copy(fields.at[slot], out, sem)
    copy.start()
    copy.wait()


def take(slot, fields, *earlier):
    return pl.pallas_call(
        functools.partial(take_kernel, slot),
        out_shape=jax.ShapeDtypeStruct(fields.shape[1:], F32),
        in_specs=[HBM] * (1 + len(earlier)),
        out_specs=VMEM,
        scratch_shapes=[pltpu.SemaphoreType.DMA],
        compiler_params=pltpu.CompilerParams(vmem_limit_bytes=SCOPED),
        cost_estimate=pl.CostEstimate(flops=0, bytes_accessed=1600000, transcendentals=0),
    )(fields, *earlier)


def gate_kernel(*refs):
    pass


def gate(block, *earlier):
    return pl.pallas_call(
        gate_kernel,
        out_shape=jax.ShapeDtypeStruct(block.shape, F32),
        in_specs=[HBM] * (1 + len(earlier)),
        out_specs=HBM,
        input_output_aliases={0: 0},
        compiler_params=pltpu.CompilerParams(vmem_limit_bytes=SCOPED),
        cost_estimate=pl.CostEstimate(flops=0, bytes_accessed=4096, transcendentals=0),
    )(block, *earlier)


def cut_kernel(many, plan, *rest):
    blocks, inner = rest[:many], rest[-1]
    cells, rows, _ = blocks[0].shape
    second = plan[SECOND] == 1
    for i, block in enumerate(blocks):

        def rim(x, carry):
            inner[i, x] = jnp.where(second, block[x, 0:2], block[x, rows - 2 : rows])
            return carry

        lax.fori_loop(0, cells, rim, 0, unroll=4)


def cut(plan, blocks, earlier):
    cells, _, depth = blocks[0].shape
    return pl.pallas_call(
        functools.partial(cut_kernel, len(blocks)),
        out_shape=jax.ShapeDtypeStruct((len(blocks), cells, 2, depth), F32),
        in_specs=[SMEM] + [VMEM] * len(blocks) + [HBM] * len(earlier),
        out_specs=VMEM,
        compiler_params=pltpu.CompilerParams(vmem_limit_bytes=SCOPED),
        cost_estimate=pl.CostEstimate(flops=0, bytes_accessed=1000000, transcendentals=0),
    )(plan, *blocks, *earlier)


def image_kernel(
    slot, spot, plan, weights, fields, near, far, own_twin, own_edge, near_twin, near_edge, far_twin, far_edge, *rest
):
    to_source, to_receiver, token, ext, prod, mix, mext, done, sems = rest[-9:]
    _, cells, rows, depth = fields.shape
    halves = ext.shape[0]
    lanes = depth // halves
    pairs = to_source.shape[0]
    taps = weights.shape[0] // pairs
    odd, second = plan[ODD], plan[SECOND] == 1
    near_at = jnp.where(odd == 1, 0, 2 * cells)
    far_at = 2 * cells - near_at
    first, last = plan[FIRST + slot], plan[FIRST + slot + 1]
    part = [slice(z * lanes, (z + 1) * lanes) for z in range(halves)]
    low_tile = lax.broadcasted_iota(jnp.int32, (8, lanes), 0)

    def widen(target, at, block, twin, edge):
        def one(x, carry):
            for z in range(halves):
                t, e = twin[x, :, part[z]], edge[x, :, part[z]]
                target[z, at + x, 8 : rows + 8] = block[x, :, part[z]]
                target[z, at + x, 6:8] = jnp.where(second, t, e)
                target[z, at + x, rows + 8 : rows + 10] = jnp.where(second, e, t)
            return carry

        lax.fori_loop(0, cells, one, 0, unroll=4)

    widen(ext, cells, fields.at[slot], own_twin.at[slot], own_edge.at[slot])
    widen(ext, near_at, near, near_twin.at[0], near_edge.at[slot])
    widen(ext, far_at, far, far_twin.at[spot], far_edge.at[slot])

    def product(x, carry):
        for z in range(halves):
            e, q = ext.at[z, x], prod.at[z, x]
            here = e[8 : rows + 8]
            q[0:rows] = here * here
            q[rows : 2 * rows] = here * e[9 : rows + 9]
            q[2 * rows : 3 * rows] = here * e[10 : rows + 10]
            base = e[0:8]
            one = base * e[1:9]
            two = base * e[2:10]
            q[3 * rows : 3 * rows + 8] = jnp.where(low_tile >= 6, two, pltpu.roll(one, 6, 0))
        return carry

    lax.fori_loop(0, 3 * cells, product, 0, unroll=4)

    def unit(index, carry):
        i = index - first
        u = plan[ORDER + index]
        to_r = lax.rem(u, 2)
        p = lax.div(u, 2)
        mate = plan[SLOT + u + 1 - 2 * to_r]
        sign = 1 - 2 * to_r
        at = [cells + sign * plan[LAG + h] for h in range(taps)]
        scale = [weights[p * taps + h] for h in range(taps)]
        widen(mext, 0, fields.at[mate], own_twin.at[mate], own_edge.at[mate])

        def total(x, carry):
            for z in range(halves):
                m, s = mix.at[z], mext.at[z, x]
                acc = None
                for h in range(taps):
                    term = scale[h] * prod[z, x + at[h]]
                    acc = term if acc is None else acc + term
                m[0, 8 : rows + 8] = acc[rows : 2 * rows]
                m[1, 8 : rows + 8] = acc[2 * rows : 3 * rows]
                extra = acc[3 * rows : 3 * rows + 8]
                m[0, 0:8] = pltpu.roll(extra, 2, 0)
                m[1, 0:8] = extra
                one = acc[rows : 2 * rows] * s[9 : rows + 9] + m[0, 7 : rows + 7] * s[7 : rows + 7]
                two = acc[2 * rows : 3 * rows] * s[10 : rows + 10] + m[1, 6 : rows + 6] * s[6 : rows + 6]
                done[i, x, :, part[z]] = 0.375 * (acc[0:rows] * s[8 : rows + 8]) + 0.25 * one + 0.0625 * two
            return carry

        lax.fori_loop(0, cells, total, 0)
        for which, target in enumerate((to_source, to_receiver)):

            @pl.when(to_r == which)
            def _():
                pltpu.make_async_copy(done.at[i], target.at[p], sems.at[i]).start()

        return carry

    lax.fori_loop(first, last, unit, 0)

    def settle(index, carry):
        i = index - first
        pltpu.make_async_copy(done.at[i], to_source.at[0], sems.at[i]).wait()
        return carry

    lax.fori_loop(first, last, settle, 0)
    token[...] = jnp.zeros_like(token)


def image(slot, pairs, plan, weights, fields, near, far, halos, spot, outs):
    _, cells, rows, depth = fields.shape
    whole = jax.ShapeDtypeStruct((pairs, cells, rows, depth), F32)
    halves = 2
    lanes = depth // halves
    return pl.pallas_call(
        functools.partial(image_kernel, slot, spot),
        out_shape=[whole, whole, jax.ShapeDtypeStruct((8, 128), F32)],
        in_specs=[SMEM] * 2 + [VMEM] * 9 + [MAIN] * len(outs),
        out_specs=[MAIN, MAIN, VMEM],
        input_output_aliases={11 + i: i for i in range(len(outs))},
        scratch_shapes=[
            pltpu.VMEM((halves, 3 * cells, rows + 16, lanes), F32),
            pltpu.VMEM((halves, 3 * cells, 3 * rows + 8, lanes), F32),
            pltpu.VMEM((halves, 2, rows + 8, lanes), F32),
            pltpu.VMEM((halves, cells, rows + 16, lanes), F32),
            pltpu.VMEM((pairs, cells, rows, depth), F32),
            pltpu.SemaphoreType.DMA((pairs,)),
        ],
        compiler_params=pltpu.CompilerParams(vmem_limit_bytes=SCOPED),
        cost_estimate=pl.CostEstimate(flops=22 * 10**6, bytes_accessed=22 * 10**6, transcendentals=0),
    )(plan, weights, fields, near, far, *halos, *outs)


def work(count, pairs, routes, plan, weights, source, receiver):
    send = lambda value, route: lax.ppermute(value, ("gx", "gy"), routes[route])

    near = [send(lead(plan, source, receiver), "across")]
    fields, inner, outer = gather(plan, source, receiver, count)
    own_twin = send(inner, "twins")
    own_edge = send(outer, "seam")
    near_edge = send(outer, "seam_near")
    far_edge = send(outer, "seam_far")
    near.append(send(take(1, fields, own_twin, own_edge, near_edge), "across"))

    far, twins, tokens = [], [], []
    outs = ()
    for s in range(count + 1):
        if s < count:
            if s >= 2:
                near[s] = gate(near[s], tokens[s - 2])
            far.append(send(near[s], "onward"))
            if s + 2 < count:
                earlier = [near[s], far_edge] if s == 0 else [near[s], far[s - 1], twins[s - 1]]
                earlier = earlier + tokens[s - 2 : s - 1] if s >= 2 else earlier
                near.append(send(take(s + 2, fields, *earlier), "across"))
        blocks = near[s : s + 1] + (far[s - 1 : s] if s >= 1 else [])
        twins.append(send(cut(plan, blocks, tokens[s - 2 : s - 1] if s >= 2 else []), "twins"))
        if s >= 1:
            halos = (own_twin, own_edge, twins[s - 1], near_edge, twins[s], far_edge)
            *outs, token = image(s - 1, pairs, plan, weights, fields, near[s - 1], far[s - 1], halos, len(blocks) - 1, outs)
            tokens.append(token)
    return tuple(outs)


def local(routes, source_snaps, receiver_snaps, snap_pairs, offset_lags, weight_table, weight_index):
    pairs = snap_pairs.shape[0]
    plan, weights = pl.pallas_call(
        functools.partial(plan_kernel, receiver_snaps.shape[0]),
        out_shape=[
            jax.ShapeDtypeStruct((LAG + offset_lags.shape[0],), jnp.int32),
            jax.ShapeDtypeStruct((pairs * offset_lags.shape[0],), F32),
        ],
        in_specs=[SMEM] * 4,
        out_specs=[SMEM] * 2,
    )(snap_pairs, offset_lags, weight_table, weight_index)
    least = 2
    most = 2 * pairs
    branches = [functools.partial(work, count, pairs, routes) for count in range(least, most + 1)]
    return lax.switch(plan[COUNT] - least, branches, plan, weights, source_snaps, receiver_snaps)


def solution(mesh):
    routes = moves(mesh)
    split = P(None, "gx", "gy", None)
    return jax.shard_map(
        functools.partial(local, routes),
        mesh=mesh,
        in_specs=(split, split, P(), P(), P(), P()),
        out_specs=(split, split),
        check_vma=False,
    )
```

```python
import functools

import jax
import jax.numpy as jnp
from jax import lax
from jax.experimental import pallas as pl
from jax.experimental.pallas import tpu as pltpu
from jax.sharding import PartitionSpec as P

F32 = jnp.float32
SMEM = pl.BlockSpec(memory_space=pltpu.SMEM)
VMEM = pl.BlockSpec(memory_space=pltpu.VMEM)
HBM = pl.BlockSpec(memory_space=pl.ANY)
SCOPED = 24 * 2**20

ODD, SECOND, COUNT, FIELD, SLOT, FIRST, ORDER, LAG = 0, 1, 2, 8, 16, 24, 32, 40


def moves(mesh):
    nx, ny = mesh.shape["gx"], mesh.shape["gy"]
    flat = lambda x, y: x * ny + y
    across = [(x, x ^ 1) for x in range(nx) if x ^ 1 < nx]
    onward = [(x, x + 2) for x in range(0, nx - 2, 2)] + [(x, x - 2) for x in range(3, nx, 2)]
    whole = lambda route, rows: [(flat(a, y), flat(b, y)) for a, b in route for y in rows]
    seams = [(a, b) for y in range(1, ny - 1, 2) for a, b in ((y, y + 1), (y + 1, y))]
    return {
        "across": whole(across, range(ny)),
        "onward": whole(onward, range(ny)),
        "twins": [(flat(x, y), flat(x, y ^ 1)) for x in range(nx) for y in range(ny)],
        "seam": [(flat(x, a), flat(x, b)) for x in range(nx) for a, b in seams],
        "seam_near": [(flat(x, a), flat(t, b)) for x, t in across for a, b in seams],
        "seam_far": [(flat(x ^ 1, a), flat(t, b)) for x, t in onward for a, b in seams],
    }


def plan_kernel(snaps, pairs, lags, table, rows, plan, weights):
    units = 2 * pairs.shape[0]
    plan[ODD] = lax.rem(lax.axis_index("gx"), 2)
    plan[SECOND] = lax.rem(lax.axis_index("gy"), 2)
    ids = [pairs[u // 2, 1] if u % 2 == 0 else pairs[u // 2, 0] + snaps for u in range(units)]
    same = [[(ids[u] == ids[v]).astype(jnp.int32) for v in range(units)] for u in range(units)]
    uses = [sum(same[u]) for u in range(units)]
    leads = [jnp.int32(1)]
    for u in range(1, units):
        leads.append((sum(same[u][:u]) == 0).astype(jnp.int32))
    rank = []
    for u in range(units):
        ahead = jnp.int32(0)
        for v in range(units):
            if v != u:
                sooner = uses[v] >= uses[u] if v < u else uses[v] > uses[u]
                ahead = ahead + leads[v] * sooner.astype(jnp.int32)
        rank.append(ahead)
    slots = [sum(same[u][v] * leads[v] * rank[v] for v in range(units)) for u in range(units)]
    plan[COUNT] = sum(leads)
    for u in range(units):
        plan[SLOT + u] = slots[u]
        plan[FIELD + slots[u]] = ids[u]
        before = jnp.int32(0)
        for v in range(units):
            if v != u:
                sooner = slots[v] <= slots[u] if v < u else slots[v] < slots[u]
                before = before + sooner.astype(jnp.int32)
        plan[ORDER + before] = u
        plan[FIRST + u] = sum((slots[v] < u).astype(jnp.int32) for v in range(units))
    plan[FIRST + units] = units
    for h in range(lags.shape[0]):
        plan[LAG + h] = 2 * lags[h]
        for p in range(pairs.shape[0]):
            weights[p * lags.shape[0] + h] = table[rows[p], h]


def launch(kernel, inputs, outputs, scratch, earlier, aliases=None):
    begin, end = len(inputs), len(inputs) + len(earlier)

    def body(*refs):
        results = refs[end : end + len(outputs)]
        token = refs[end + len(outputs)]
        kernel(*refs[:begin], *results, *refs[end + len(outputs) + 1 :])
        token[...] = jnp.zeros_like(token)

    return pl.pallas_call(
        body,
        out_shape=[shape for shape, _ in outputs] + [jax.ShapeDtypeStruct((8, 128), F32)],
        in_specs=[memory for _, memory in inputs] + [HBM] * len(earlier),
        out_specs=[memory for _, memory in outputs] + [VMEM],
        scratch_shapes=scratch,
        input_output_aliases=aliases or {},
        compiler_params=pltpu.CompilerParams(vmem_limit_bytes=SCOPED),
        cost_estimate=pl.CostEstimate(flops=0, bytes_accessed=2000000, transcendentals=0),
    )(*[array for array, _ in inputs], *earlier)


def fetch(field, source, receiver, target, sem):
    snaps = receiver.shape[0]
    width = pl.ds(0, target.shape[-1])

    @pl.when(field < snaps)
    def _():
        pltpu.make_async_copy(receiver.at[jnp.minimum(field, snaps - 1), :, :, width], target, sem).start()

    @pl.when(field >= snaps)
    def _():
        pltpu.make_async_copy(source.at[jnp.maximum(field - snaps, 0), :, :, width], target, sem).start()

    return pltpu.make_async_copy(receiver.at[0, :, :, width], target, sem)


def lead_kernel(plan, source, receiver, out, sem):
    fetch(plan[FIELD], source, receiver, out, sem).wait()


def lead(plan, source, receiver, width):
    block = jax.ShapeDtypeStruct(source.shape[1:3] + (width,), F32)
    inputs = [(plan, SMEM), (source, HBM), (receiver, HBM)]
    return launch(lead_kernel, inputs, [(block, VMEM)], [pltpu.SemaphoreType.DMA], [])


def gather_kernel(plan, source, receiver, fields, inner, outer, sems):
    count, cells, rows, _ = fields.shape
    waits = [fetch(plan[FIELD + s], source, receiver, fields.at[s], sems.at[s]) for s in range(count)]
    second = plan[SECOND] == 1
    for s, wait in enumerate(waits):
        wait.wait()

        def rim(x, carry):
            low, high = fields[s, x, 0:2], fields[s, x, rows - 2 : rows]
            inner[s, x] = jnp.where(second, low, high)
            outer[s, x] = jnp.where(second, high, low)
            return carry

        lax.fori_loop(0, cells, rim, 0, unroll=4)


def gather(plan, source, receiver, count, earlier):
    _, cells, rows, depth = source.shape
    edge = jax.ShapeDtypeStruct((count, cells, 2, depth), F32)
    whole = jax.ShapeDtypeStruct((count, cells, rows, depth), F32)
    inputs = [(plan, SMEM), (source, HBM), (receiver, HBM)]
    outputs = [(whole, VMEM), (edge, VMEM), (edge, VMEM)]
    return launch(gather_kernel, inputs, outputs, [pltpu.SemaphoreType.DMA((count,))], earlier)


def take_kernel(piece, fields, out, sem):
    slot, start, width = piece
    copy = pltpu.make_async_copy(fields.at[slot, :, :, pl.ds(start, width)], out, sem)
    copy.start()
    copy.wait()


def take(piece, fields, earlier):
    block = jax.ShapeDtypeStruct(fields.shape[1:3] + piece[2:], F32)
    kernel = functools.partial(take_kernel, piece)
    return launch(kernel, [(fields, HBM)], [(block, VMEM)], [pltpu.SemaphoreType.DMA], earlier)


def turn_kernel(piece, block, fields, same, out, sem):
    take_kernel(piece, fields, out, sem)


def turn(block, piece, fields, earlier):
    shape = jax.ShapeDtypeStruct(block.shape, F32)
    out = jax.ShapeDtypeStruct(fields.shape[1:3] + piece[2:], F32)
    kernel = functools.partial(turn_kernel, piece)
    outputs = [(shape, HBM), (out, VMEM)]
    return launch(kernel, [(block, HBM), (fields, HBM)], outputs, [pltpu.SemaphoreType.DMA], earlier, {0: 0})


def gate_kernel(block, same):
    pass


def gate(block, earlier):
    shape = jax.ShapeDtypeStruct(block.shape, F32)
    return launch(gate_kernel, [(block, HBM)], [(shape, HBM)], [], earlier, {0: 0})


def cut_kernel(many, plan, *rest):
    blocks, inner = rest[:many], rest[many]
    cells, rows, _ = blocks[0].shape
    second = plan[SECOND] == 1
    start = 0
    for block in blocks:
        lanes = slice(start, start + block.shape[2])
        start = lanes.stop

        def rim(x, carry):
            inner[x, :, lanes] = jnp.where(second, block[x, 0:2], block[x, rows - 2 : rows])
            return carry

        lax.fori_loop(0, cells, rim, 0, unroll=4)


def cut_type(blocks):
    return jax.ShapeDtypeStruct((blocks[0].shape[0], 2, sum(block.shape[2] for block in blocks)), F32)


def cut(plan, blocks, earlier):
    inputs = [(plan, SMEM)] + [(block, VMEM) for block in blocks]
    return launch(functools.partial(cut_kernel, len(blocks)), inputs, [(cut_type(blocks), VMEM)], [], earlier)


def image_kernel(
    piece, spot, plan, weights, fields, near, far, own_twin, own_edge, near_twin, near_edge, far_twin, far_edge, *rest
):
    to_source, to_receiver, ext, prod, mix, mext, done, sems = rest[-8:]
    slot, start, _ = piece
    _, cells, rows, _ = fields.shape
    halves, lanes = ext.shape[0], ext.shape[3]
    pairs = to_source.shape[0]
    taps = weights.shape[0] // pairs
    odd, second = plan[ODD], plan[SECOND] == 1
    near_at = jnp.where(odd == 1, 0, 2 * cells)
    far_at = 2 * cells - near_at
    first, last = plan[FIRST + slot], plan[FIRST + slot + 1]
    part = [slice(z * lanes, (z + 1) * lanes) for z in range(halves)]
    whole = [slice(start + z * lanes, start + (z + 1) * lanes) for z in range(halves)]
    passed = [slice(spot + z * lanes, spot + (z + 1) * lanes) for z in range(halves)]
    low_tile = lax.broadcasted_iota(jnp.int32, (8, lanes), 0)

    def widen(target, at, block, block_lanes, twin, twin_lanes, edge):
        def one(x, carry):
            for z in range(halves):
                t, e = twin[x, :, twin_lanes[z]], edge[x, :, whole[z]]
                target[z, at + x, 8 : rows + 8] = block[x, :, block_lanes[z]]
                target[z, at + x, 6:8] = jnp.where(second, t, e)
                target[z, at + x, rows + 8 : rows + 10] = jnp.where(second, e, t)
            return carry

        lax.fori_loop(0, cells, one, 0, unroll=4)

    widen(ext, cells, fields.at[slot], whole, own_twin.at[slot], whole, own_edge.at[slot])
    widen(ext, near_at, near, part, near_twin, part, near_edge.at[slot])
    widen(ext, far_at, far, part, far_twin, passed, far_edge.at[slot])

    def product(x, carry):
        for z in range(halves):
            e, q = ext.at[z, x], prod.at[z, x]
            here = e[8 : rows + 8]
            q[0:rows] = here * here
            q[rows : 2 * rows] = here * e[9 : rows + 9]
            q[2 * rows : 3 * rows] = here * e[10 : rows + 10]
            base = e[0:8]
            one = base * e[1:9]
            two = base * e[2:10]
            q[3 * rows : 3 * rows + 8] = jnp.where(low_tile >= 6, two, pltpu.roll(one, 6, 0))
        return carry

    lax.fori_loop(0, 3 * cells, product, 0, unroll=4)

    def window(target, p):
        return target.at[p, :, :, pl.ds(start, halves * lanes)]

    def unit(index, carry):
        i = index - first
        u = plan[ORDER + index]
        to_r = lax.rem(u, 2)
        p = lax.div(u, 2)
        mate = plan[SLOT + u + 1 - 2 * to_r]
        sign = 1 - 2 * to_r
        at = [cells + sign * plan[LAG + h] for h in range(taps)]
        scale = [weights[p * taps + h] for h in range(taps)]
        widen(mext, 0, fields.at[mate], whole, own_twin.at[mate], whole, own_edge.at[mate])

        def total(x, carry):
            for z in range(halves):
                m, s = mix.at[z], mext.at[z, x]
                acc = None
                for h in range(taps):
                    term = scale[h] * prod[z, x + at[h]]
                    acc = term if acc is None else acc + term
                m[0, 8 : rows + 8] = acc[rows : 2 * rows]
                m[1, 8 : rows + 8] = acc[2 * rows : 3 * rows]
                extra = acc[3 * rows : 3 * rows + 8]
                m[0, 0:8] = pltpu.roll(extra, 2, 0)
                m[1, 0:8] = extra
                one = acc[rows : 2 * rows] * s[9 : rows + 9] + m[0, 7 : rows + 7] * s[7 : rows + 7]
                two = acc[2 * rows : 3 * rows] * s[10 : rows + 10] + m[1, 6 : rows + 6] * s[6 : rows + 6]
                done[i, x, :, part[z]] = 0.375 * (acc[0:rows] * s[8 : rows + 8]) + 0.25 * one + 0.0625 * two
            return carry

        lax.fori_loop(0, cells, total, 0)
        for which, target in enumerate((to_source, to_receiver)):

            @pl.when(to_r == which)
            def _():
                pltpu.make_async_copy(done.at[i], window(target, p), sems.at[i]).start()

        return carry

    lax.fori_loop(first, last, unit, 0)

    def settle(index, carry):
        i = index - first
        pltpu.make_async_copy(done.at[i], window(to_source, 0), sems.at[i]).wait()
        return carry

    lax.fori_loop(first, last, settle, 0)


def joint_kernel(many, piece, spot, news, *refs):
    plan, blocks, begin = refs[0], refs[1 : 1 + many], 1 + many
    results = refs[begin + 10 + news :]
    if many:
        cut_kernel(many, plan, *blocks, results[0])
        results = results[1:]
    image_kernel(piece, spot, plan, *refs[begin : begin + 10], *results)


def image(blocks, piece, pairs, plan, weights, fields, near, far, halos, spot, outs, earlier):
    _, cells, rows, depth = fields.shape
    whole = jax.ShapeDtypeStruct((pairs, cells, rows, depth), F32)
    lanes = 128 if piece[2] % 128 == 0 else piece[2]
    halves = piece[2] // lanes
    inputs = [(plan, SMEM)] + [(block, VMEM) for block in blocks]
    inputs += [(weights, SMEM), (fields, VMEM), (near, VMEM), (far, VMEM)] + [(halo, VMEM) for halo in halos]
    first = len(inputs)
    inputs += [(out, HBM) for out in outs]
    outputs = ([(cut_type(blocks), VMEM)] if blocks else []) + [(whole, HBM), (whole, HBM)]
    scratch = [
        pltpu.VMEM((halves, 3 * cells, rows + 16, lanes), F32),
        pltpu.VMEM((halves, 3 * cells, 3 * rows + 8, lanes), F32),
        pltpu.VMEM((halves, 2, rows + 8, lanes), F32),
        pltpu.VMEM((halves, cells, rows + 16, lanes), F32),
        pltpu.VMEM((pairs, cells, rows, halves * lanes), F32),
        pltpu.SemaphoreType.DMA((pairs,)),
    ]
    kernel = functools.partial(joint_kernel, len(blocks), piece, spot, len(outs))
    aliases = {first + i: len(outputs) - 2 + i for i in range(len(outs))}
    return launch(kernel, inputs, outputs, scratch, earlier, aliases)


AHEAD, TWINS = 2, 1
SPLIT_FIRST, SPLIT_LAST = False, False


def pieces_of(count, depth):
    pieces = []
    for slot in range(count):
        halved = depth % 256 == 0 and ((SPLIT_LAST and slot == count - 1) or (SPLIT_FIRST and slot == 0))
        width = depth // 2 if halved else depth
        pieces += [(slot, start, width) for start in range(0, depth, width)]
    return pieces


def work(count, pairs, routes, plan, weights, source, receiver):
    send = lambda value, route: lax.ppermute(value, ("gx", "gy"), routes[route])
    pieces = pieces_of(count, source.shape[3])
    last = len(pieces)

    first, token = lead(plan, source, receiver, pieces[0][2])
    near = [send(first, "across")]
    fields, inner, outer, token = gather(plan, source, receiver, count, [token])
    own_edge = send(outer, "seam")
    near_edge = send(outer, "seam_near")
    far_edge = send(outer, "seam_far")
    own_twin = send(inner, "twins")
    earlier = [own_twin, own_edge, near_edge]
    for piece in pieces[1:AHEAD]:
        block, token = take(piece, fields, [token] + earlier)
        near.append(send(block, "across"))
        earlier = []

    far, twins, outs = [], [], ()

    def sums(blocks, k, outs, token):
        halos = (own_twin, own_edge, twins[k], near_edge, twins[k + 1], far_edge)
        spot = pieces[k + 1][2] if k + 1 < last else 0
        *edge, to_source, to_receiver, token = image(
            blocks, pieces[k], pairs, plan, weights, fields, near[k], far[k], halos, spot, outs, [token]
        )
        return edge, (to_source, to_receiver), token

    for k in range(last):
        earlier = [token] + ([far_edge] if k == 0 else twins[k - TWINS : k - TWINS + 1] if TWINS <= k else [])
        if k + AHEAD < last:
            near[k], block, token = turn(near[k], pieces[k + AHEAD], fields, earlier)
            near.append(send(block, "across"))
        else:
            near[k], token = gate(near[k], earlier)
        far.append(send(near[k], "onward"))
        blocks = near[k : k + 1] + (far[k - 1 : k] if k >= 1 else [])
        if k < 2:
            edge, token = cut(plan, blocks, [token])
        else:
            (edge,), outs, token = sums(blocks, k - 2, outs, token)
        twins.append(send(edge, "twins"))
    _, outs, token = sums([], last - 2, outs, token)
    edge, token = cut(plan, far[last - 1 :], [token])
    twins.append(send(edge, "twins"))
    _, outs, token = sums([], last - 1, outs, token)
    return outs


def local(routes, source_snaps, receiver_snaps, snap_pairs, offset_lags, weight_table, weight_index):
    pairs = snap_pairs.shape[0]
    plan, weights = pl.pallas_call(
        functools.partial(plan_kernel, receiver_snaps.shape[0]),
        out_shape=[
            jax.ShapeDtypeStruct((LAG + offset_lags.shape[0],), jnp.int32),
            jax.ShapeDtypeStruct((pairs * offset_lags.shape[0],), F32),
        ],
        in_specs=[SMEM] * 4,
        out_specs=[SMEM] * 2,
    )(snap_pairs, offset_lags, weight_table, weight_index)
    least = 2
    most = 2 * pairs
    branches = [functools.partial(work, count, pairs, routes) for count in range(least, most + 1)]
    return lax.switch(plan[COUNT] - least, branches, plan, weights, source_snaps, receiver_snaps)


def solution(mesh):
    routes = moves(mesh)
    split = P(None, "gx", "gy", None)
    return jax.shard_map(
        functools.partial(local, routes),
        mesh=mesh,
        in_specs=(split, split, P(), P(), P(), P()),
        out_specs=(split, split),
        check_vma=False,
    )
```

```python
import functools

import jax
import jax.numpy as jnp
from jax import lax
from jax.experimental import pallas as pl
from jax.experimental.pallas import tpu as pltpu
from jax.sharding import PartitionSpec as P

F32 = jnp.float32
SMEM = pl.BlockSpec(memory_space=pltpu.SMEM)
VMEM = pl.BlockSpec(memory_space=pltpu.VMEM)
HBM = pl.BlockSpec(memory_space=pl.ANY)
SCOPED = 24 * 2**20

ODD, SECOND, FIELD, SLOT, FIRST, ORDER, LAG = 0, 1, 8, 16, 24, 32, 40


def moves(mesh):
    nx, ny = mesh.shape["gx"], mesh.shape["gy"]
    flat = lambda x, y: x * ny + y
    across = [(x, x ^ 1) for x in range(nx) if x ^ 1 < nx]
    onward = [(x, x + 2) for x in range(0, nx - 2, 2)] + [(x, x - 2) for x in range(3, nx, 2)]
    whole = lambda route, rows: [(flat(a, y), flat(b, y)) for a, b in route for y in rows]
    seams = [(a, b) for y in range(1, ny - 1, 2) for a, b in ((y, y + 1), (y + 1, y))]
    return {
        "across": whole(across, range(ny)),
        "onward": whole(onward, range(ny)),
        "twins": [(flat(x, y), flat(x, y ^ 1)) for x in range(nx) for y in range(ny)],
        "seam": [(flat(x, a), flat(x, b)) for x in range(nx) for a, b in seams],
        "seam_near": [(flat(x, a), flat(t, b)) for x, t in across for a, b in seams],
        "seam_far": [(flat(x ^ 1, a), flat(t, b)) for x, t in onward for a, b in seams],
    }


def plan_kernel(snaps, least, pairs, lags, table, rows, plan, weights, branch):
    units = 2 * pairs.shape[1]
    plan[ODD] = lax.rem(lax.axis_index("gx"), 2)
    plan[SECOND] = lax.rem(lax.axis_index("gy"), 2)
    ids = [pairs[1, u // 2] if u % 2 == 0 else pairs[0, u // 2] + snaps for u in range(units)]
    same = [[(ids[u] == ids[v]).astype(jnp.int32) for v in range(units)] for u in range(units)]
    uses = [sum(same[u]) for u in range(units)]
    leads = [jnp.int32(1)]
    for u in range(1, units):
        leads.append((sum(same[u][:u]) == 0).astype(jnp.int32))
    rank = []
    for u in range(units):
        ahead = jnp.int32(0)
        for v in range(units):
            if v != u:
                sooner = uses[v] >= uses[u] if v < u else uses[v] > uses[u]
                ahead = ahead + leads[v] * sooner.astype(jnp.int32)
        rank.append(ahead)
    slots = [sum(same[u][v] * leads[v] * rank[v] for v in range(units)) for u in range(units)]
    branch[0] = sum(leads) - least
    for u in range(units):
        plan[SLOT + u] = slots[u]
        plan[FIELD + slots[u]] = ids[u]
        before = jnp.int32(0)
        for v in range(units):
            if v != u:
                sooner = slots[v] <= slots[u] if v < u else slots[v] < slots[u]
                before = before + sooner.astype(jnp.int32)
        plan[ORDER + before] = u
        plan[FIRST + u] = sum((slots[v] < u).astype(jnp.int32) for v in range(units))
    plan[FIRST + units] = units
    for h in range(lags.shape[0]):
        plan[LAG + h] = 2 * lags[h]
        for p in range(pairs.shape[1]):
            weights[p * lags.shape[0] + h] = table[rows[p], h]


def launch(kernel, inputs, outputs, scratch, earlier, aliases=None):
    begin, end = len(inputs), len(inputs) + len(earlier)

    def body(*refs):
        results = refs[end : end + len(outputs)]
        token = refs[end + len(outputs)]
        kernel(*refs[:begin], *results, *refs[end + len(outputs) + 1 :])
        token[...] = jnp.zeros_like(token)

    return pl.pallas_call(
        body,
        out_shape=[shape for shape, _ in outputs] + [jax.ShapeDtypeStruct((8, 128), F32)],
        in_specs=[memory for _, memory in inputs] + [HBM] * len(earlier),
        out_specs=[memory for _, memory in outputs] + [VMEM],
        scratch_shapes=scratch,
        input_output_aliases=aliases or {},
        compiler_params=pltpu.CompilerParams(vmem_limit_bytes=SCOPED),
        cost_estimate=pl.CostEstimate(flops=0, bytes_accessed=2000000, transcendentals=0),
    )(*[array for array, _ in inputs], *earlier)


def fetch(field, source, receiver, target, sem):
    snaps = receiver.shape[0]
    width = pl.ds(0, target.shape[-1])

    @pl.when(field < snaps)
    def _():
        pltpu.make_async_copy(receiver.at[jnp.minimum(field, snaps - 1), :, :, width], target, sem).start()

    @pl.when(field >= snaps)
    def _():
        pltpu.make_async_copy(source.at[jnp.maximum(field - snaps, 0), :, :, width], target, sem).start()

    return pltpu.make_async_copy(receiver.at[0, :, :, width], target, sem)


def lead_kernel(plan, source, receiver, out, sem):
    fetch(plan[FIELD], source, receiver, out, sem).wait()


def lead(plan, source, receiver, width):
    block = jax.ShapeDtypeStruct(source.shape[1:3] + (width,), F32)
    inputs = [(plan, SMEM), (source, HBM), (receiver, HBM)]
    return launch(lead_kernel, inputs, [(block, VMEM)], [pltpu.SemaphoreType.DMA], [])


def gather_kernel(plan, source, receiver, fields, inner, outer, sems):
    count, cells, rows, _ = fields.shape
    waits = [fetch(plan[FIELD + s], source, receiver, fields.at[s], sems.at[s]) for s in range(count)]
    second = plan[SECOND] == 1
    for s, wait in enumerate(waits):
        wait.wait()

        def rim(x, carry):
            low, high = fields[s, x, 0:2], fields[s, x, rows - 2 : rows]
            inner[s, x] = jnp.where(second, low, high)
            outer[s, x] = jnp.where(second, high, low)
            return carry

        lax.fori_loop(0, cells, rim, 0, unroll=4)


def gather(plan, source, receiver, count, earlier):
    _, cells, rows, depth = source.shape
    edge = jax.ShapeDtypeStruct((count, cells, 2, depth), F32)
    whole = jax.ShapeDtypeStruct((count, cells, rows, depth), F32)
    inputs = [(plan, SMEM), (source, HBM), (receiver, HBM)]
    outputs = [(whole, VMEM), (edge, VMEM), (edge, VMEM)]
    return launch(gather_kernel, inputs, outputs, [pltpu.SemaphoreType.DMA((count,))], earlier)


def take_kernel(piece, fields, out, sem):
    slot, start, width = piece
    copy = pltpu.make_async_copy(fields.at[slot, :, :, pl.ds(start, width)], out, sem)
    copy.start()
    copy.wait()


def take(piece, fields, earlier):
    block = jax.ShapeDtypeStruct(fields.shape[1:3] + piece[2:], F32)
    kernel = functools.partial(take_kernel, piece)
    return launch(kernel, [(fields, HBM)], [(block, VMEM)], [pltpu.SemaphoreType.DMA], earlier)


def turn_kernel(piece, block, fields, same, out, sem):
    take_kernel(piece, fields, out, sem)


def turn(block, piece, fields, earlier):
    shape = jax.ShapeDtypeStruct(block.shape, F32)
    out = jax.ShapeDtypeStruct(fields.shape[1:3] + piece[2:], F32)
    kernel = functools.partial(turn_kernel, piece)
    outputs = [(shape, HBM), (out, VMEM)]
    return launch(kernel, [(block, HBM), (fields, HBM)], outputs, [pltpu.SemaphoreType.DMA], earlier, {0: 0})


def gate_kernel(block, same):
    pass


def gate(block, earlier):
    shape = jax.ShapeDtypeStruct(block.shape, F32)
    return launch(gate_kernel, [(block, HBM)], [(shape, HBM)], [], earlier, {0: 0})


def cut_kernel(many, plan, *rest):
    blocks, inner = rest[:many], rest[many]
    cells, rows, _ = blocks[0].shape
    second = plan[SECOND] == 1
    start = 0
    for block in blocks:
        lanes = slice(start, start + block.shape[2])
        start = lanes.stop

        def rim(x, carry):
            inner[x, :, lanes] = jnp.where(second, block[x, 0:2], block[x, rows - 2 : rows])
            return carry

        lax.fori_loop(0, cells, rim, 0, unroll=4)


def cut_type(blocks):
    return jax.ShapeDtypeStruct((blocks[0].shape[0], 2, sum(block.shape[2] for block in blocks)), F32)


def cut(plan, blocks, earlier):
    inputs = [(plan, SMEM)] + [(block, VMEM) for block in blocks]
    return launch(functools.partial(cut_kernel, len(blocks)), inputs, [(cut_type(blocks), VMEM)], [], earlier)


def image_kernel(
    piece, spot, plan, weights, fields, near, far, own_twin, own_edge, near_twin, near_edge, far_twin, far_edge, *rest
):
    to_source, to_receiver, ext, prod, mix, mext, done, sems = rest[-8:]
    slot, start, _ = piece
    _, cells, rows, _ = fields.shape
    halves, lanes = ext.shape[0], ext.shape[3]
    pairs = to_source.shape[0]
    taps = weights.shape[0] // pairs
    odd, second = plan[ODD], plan[SECOND] == 1
    near_at = jnp.where(odd == 1, 0, 2 * cells)
    far_at = 2 * cells - near_at
    first, last = plan[FIRST + slot], plan[FIRST + slot + 1]
    part = [slice(z * lanes, (z + 1) * lanes) for z in range(halves)]
    whole = [slice(start + z * lanes, start + (z + 1) * lanes) for z in range(halves)]
    passed = [slice(spot + z * lanes, spot + (z + 1) * lanes) for z in range(halves)]
    low_tile = lax.broadcasted_iota(jnp.int32, (8, lanes), 0)

    def widen(target, at, block, block_lanes, twin, twin_lanes, edge):
        def one(x, carry):
            for z in range(halves):
                t, e = twin[x, :, twin_lanes[z]], edge[x, :, whole[z]]
                target[z, at + x, 8 : rows + 8] = block[x, :, block_lanes[z]]
                target[z, at + x, 6:8] = jnp.where(second, t, e)
                target[z, at + x, rows + 8 : rows + 10] = jnp.where(second, e, t)
            return carry

        lax.fori_loop(0, cells, one, 0, unroll=4)

    widen(ext, cells, fields.at[slot], whole, own_twin.at[slot], whole, own_edge.at[slot])
    widen(ext, near_at, near, part, near_twin, part, near_edge.at[slot])
    widen(ext, far_at, far, part, far_twin, passed, far_edge.at[slot])

    def product(x, carry):
        for z in range(halves):
            e, q = ext.at[z, x], prod.at[z, x]
            here = e[8 : rows + 8]
            q[0:rows] = here * here
            q[rows : 2 * rows] = here * e[9 : rows + 9]
            q[2 * rows : 3 * rows] = here * e[10 : rows + 10]
            base = e[0:8]
            one = base * e[1:9]
            two = base * e[2:10]
            q[3 * rows : 3 * rows + 8] = jnp.where(low_tile >= 6, two, pltpu.roll(one, 6, 0))
        return carry

    lax.fori_loop(0, 3 * cells, product, 0, unroll=4)

    def window(target, p):
        return target.at[p, :, :, pl.ds(start, halves * lanes)]

    def unit(index, carry):
        i = index - first
        u = plan[ORDER + index]
        to_r = lax.rem(u, 2)
        p = lax.div(u, 2)
        mate = plan[SLOT + u + 1 - 2 * to_r]
        sign = 1 - 2 * to_r
        at = [cells + sign * plan[LAG + h] for h in range(taps)]
        scale = [weights[p * taps + h] for h in range(taps)]
        widen(mext, 0, fields.at[mate], whole, own_twin.at[mate], whole, own_edge.at[mate])

        def total(x, carry):
            for z in range(halves):
                m, s = mix.at[z], mext.at[z, x]
                acc = None
                for h in range(taps):
                    term = scale[h] * prod[z, x + at[h]]
                    acc = term if acc is None else acc + term
                m[0, 8 : rows + 8] = acc[rows : 2 * rows]
                m[1, 8 : rows + 8] = acc[2 * rows : 3 * rows]
                extra = acc[3 * rows : 3 * rows + 8]
                m[0, 0:8] = pltpu.roll(extra, 2, 0)
                m[1, 0:8] = extra
                one = acc[rows : 2 * rows] * s[9 : rows + 9] + m[0, 7 : rows + 7] * s[7 : rows + 7]
                two = acc[2 * rows : 3 * rows] * s[10 : rows + 10] + m[1, 6 : rows + 6] * s[6 : rows + 6]
                done[i, x, :, part[z]] = 0.375 * (acc[0:rows] * s[8 : rows + 8]) + 0.25 * one + 0.0625 * two
            return carry

        lax.fori_loop(0, cells, total, 0)
        for which, target in enumerate((to_source, to_receiver)):

            @pl.when(to_r == which)
            def _():
                pltpu.make_async_copy(done.at[i], window(target, p), sems.at[i]).start()

        return carry

    lax.fori_loop(first, last, unit, 0)

    def settle(index, carry):
        i = index - first
        pltpu.make_async_copy(done.at[i], window(to_source, 0), sems.at[i]).wait()
        return carry

    lax.fori_loop(first, last, settle, 0)


def joint_kernel(many, piece, spot, news, *refs):
    plan, blocks, begin = refs[0], refs[1 : 1 + many], 1 + many
    results = refs[begin + 10 + news :]
    if many:
        cut_kernel(many, plan, *blocks, results[0])
        results = results[1:]
    image_kernel(piece, spot, plan, *refs[begin : begin + 10], *results)


def image(blocks, piece, pairs, plan, weights, fields, near, far, halos, spot, outs, earlier):
    _, cells, rows, depth = fields.shape
    whole = jax.ShapeDtypeStruct((pairs, cells, rows, depth), F32)
    lanes = 128 if piece[2] % 128 == 0 else piece[2]
    halves = piece[2] // lanes
    inputs = [(plan, SMEM)] + [(block, VMEM) for block in blocks]
    inputs += [(weights, SMEM), (fields, VMEM), (near, VMEM), (far, VMEM)] + [(halo, VMEM) for halo in halos]
    first = len(inputs)
    inputs += [(out, HBM) for out in outs]
    outputs = ([(cut_type(blocks), VMEM)] if blocks else []) + [(whole, HBM), (whole, HBM)]
    scratch = [
        pltpu.VMEM((halves, 3 * cells, rows + 16, lanes), F32),
        pltpu.VMEM((halves, 3 * cells, 3 * rows + 8, lanes), F32),
        pltpu.VMEM((halves, 2, rows + 8, lanes), F32),
        pltpu.VMEM((halves, cells, rows + 16, lanes), F32),
        pltpu.VMEM((pairs, cells, rows, halves * lanes), F32),
        pltpu.SemaphoreType.DMA((pairs,)),
    ]
    kernel = functools.partial(joint_kernel, len(blocks), piece, spot, len(outs))
    aliases = {first + i: len(outputs) - 2 + i for i in range(len(outs))}
    return launch(kernel, inputs, outputs, scratch, earlier, aliases)


AHEAD, TWINS = 2, 1
TWINFIRST = False
SOON = (4,)
SPLIT_FIRST, SPLIT_LAST = False, False


def pieces_of(count, depth):
    pieces = []
    for slot in range(count):
        halved = depth % 256 == 0 and ((SPLIT_LAST and slot == count - 1) or (SPLIT_FIRST and slot == 0))
        width = depth // 2 if halved else depth
        pieces += [(slot, start, width) for start in range(0, depth, width)]
    return pieces


def work(count, pairs, routes, plan, weights, source, receiver):
    send = lambda value, route: lax.ppermute(value, ("gx", "gy"), routes[route])
    pieces = pieces_of(count, source.shape[3])
    last = len(pieces)

    first, token = lead(plan, source, receiver, pieces[0][2])
    near = [send(first, "across")]
    fields, inner, outer, token = gather(plan, source, receiver, count, [token])
    own_twin = send(inner, "twins")
    earlier = [own_twin] if TWINFIRST else []
    for piece in pieces[1:AHEAD]:
        block, token = take(piece, fields, [token] + earlier)
        near.append(send(block, "across"))
        earlier = []
    outer, token = gate(outer, [token])
    near_edge = send(outer, "seam_near")
    far_edge = send(outer, "seam_far")
    own_edge = send(outer, "seam")

    def needed(k):
        soon = [near_edge, far_edge, own_twin] + ([own_edge] if count in SOON else [])
        return soon if k == 1 else [own_edge]

    far, twins, outs = [], [], ()

    def sums(blocks, k, outs, token):
        halos = (own_twin, own_edge, twins[k], near_edge, twins[k + 1], far_edge)
        spot = pieces[k + 1][2] if k + 1 < last else 0
        *edge, to_source, to_receiver, token = image(
            blocks, pieces[k], pairs, plan, weights, fields, near[k], far[k], halos, spot, outs, [token]
        )
        return edge, (to_source, to_receiver), token

    for k in range(last):
        earlier = [token] + (twins[k - TWINS : k - TWINS + 1] if TWINS <= k else []) + (needed(k) if k in (1, 2) else [])
        if k + AHEAD < last:
            near[k], block, token = turn(near[k], pieces[k + AHEAD], fields, earlier)
            near.append(send(block, "across"))
        else:
            near[k], token = gate(near[k], earlier)
        far.append(send(near[k], "onward"))
        blocks = near[k : k + 1] + (far[k - 1 : k] if k >= 1 else [])
        if k < 2:
            edge, token = cut(plan, blocks, [token])
        else:
            (edge,), outs, token = sums(blocks, k - 2, outs, token)
        twins.append(send(edge, "twins"))
    _, outs, token = sums([], last - 2, outs, token)
    edge, token = cut(plan, far[last - 1 :], [token])
    twins.append(send(edge, "twins"))
    _, outs, token = sums([], last - 1, outs, token)
    return outs


def local(routes, source_snaps, receiver_snaps, snap_pairs, offset_lags, weight_table, weight_index):
    pairs = snap_pairs.shape[0]
    least, most = 2, 2 * pairs
    plan, weights, branch = pl.pallas_call(
        functools.partial(plan_kernel, receiver_snaps.shape[0], least),
        out_shape=[
            jax.ShapeDtypeStruct((LAG + offset_lags.shape[0],), jnp.int32),
            jax.ShapeDtypeStruct((pairs * offset_lags.shape[0],), F32),
            jax.ShapeDtypeStruct((1,), jnp.int32),
        ],
        in_specs=[SMEM] * 4,
        out_specs=[SMEM] * 3,
    )(snap_pairs.T, offset_lags, weight_table, weight_index)
    branches = [functools.partial(work, count, pairs, routes) for count in range(least, most + 1)]
    return lax.switch(branch[0], branches, plan, weights, source_snaps, receiver_snaps)


def solution(mesh):
    routes = moves(mesh)
    split = P(None, "gx", "gy", None)
    return jax.shard_map(
        functools.partial(local, routes),
        mesh=mesh,
        in_specs=(split, split, P(), P(), P(), P()),
        out_specs=(split, split),
        check_vma=False,
    )
```

```python
import functools

import jax
import jax.numpy as jnp
from jax import lax
from jax.experimental import pallas as pl
from jax.experimental.pallas import tpu as pltpu
from jax.sharding import PartitionSpec as P

F32 = jnp.float32
SMEM = pl.BlockSpec(memory_space=pltpu.SMEM)
VMEM = pl.BlockSpec(memory_space=pltpu.VMEM)
HBM = pl.BlockSpec(memory_space=pl.ANY)
SCOPED = 24 * 2**20

ODD, SECOND, FIELD, SLOT, FIRST, ORDER, LAG = 0, 1, 8, 16, 24, 32, 40


def moves(mesh):
    nx, ny = mesh.shape["gx"], mesh.shape["gy"]
    flat = lambda x, y: x * ny + y
    across = [(x, x ^ 1) for x in range(nx) if x ^ 1 < nx]
    onward = [(x, x + 2) for x in range(0, nx - 2, 2)] + [(x, x - 2) for x in range(3, nx, 2)]
    whole = lambda route, rows: [(flat(a, y), flat(b, y)) for a, b in route for y in rows]
    seams = [(a, b) for y in range(1, ny - 1, 2) for a, b in ((y, y + 1), (y + 1, y))]
    return {
        "across": whole(across, range(ny)),
        "onward": whole(onward, range(ny)),
        "twins": [(flat(x, y), flat(x, y ^ 1)) for x in range(nx) for y in range(ny)],
        "seam": [(flat(x, a), flat(x, b)) for x in range(nx) for a, b in seams],
        "seam_near": [(flat(x, a), flat(t, b)) for x, t in across for a, b in seams],
        "seam_far": [(flat(x ^ 1, a), flat(t, b)) for x, t in onward for a, b in seams],
    }


def plan_kernel(snaps, least, pairs, lags, table, rows, plan, weights, branch):
    units = 2 * pairs.shape[1]
    plan[ODD] = lax.rem(lax.axis_index("gx"), 2)
    plan[SECOND] = lax.rem(lax.axis_index("gy"), 2)
    ids = [pairs[1, u // 2] if u % 2 == 0 else pairs[0, u // 2] + snaps for u in range(units)]
    same = [[(ids[u] == ids[v]).astype(jnp.int32) for v in range(units)] for u in range(units)]
    uses = [sum(same[u]) for u in range(units)]
    leads = [jnp.int32(1)]
    for u in range(1, units):
        leads.append((sum(same[u][:u]) == 0).astype(jnp.int32))
    rank = []
    for u in range(units):
        ahead = jnp.int32(0)
        for v in range(units):
            if v != u:
                sooner = uses[v] >= uses[u] if v < u else uses[v] > uses[u]
                ahead = ahead + leads[v] * sooner.astype(jnp.int32)
        rank.append(ahead)
    slots = [sum(same[u][v] * leads[v] * rank[v] for v in range(units)) for u in range(units)]
    branch[0] = sum(leads) - least
    for u in range(units):
        plan[SLOT + u] = slots[u]
        plan[FIELD + slots[u]] = ids[u]
        before = jnp.int32(0)
        for v in range(units):
            if v != u:
                sooner = slots[v] <= slots[u] if v < u else slots[v] < slots[u]
                before = before + sooner.astype(jnp.int32)
        plan[ORDER + before] = u
        plan[FIRST + u] = sum((slots[v] < u).astype(jnp.int32) for v in range(units))
    plan[FIRST + units] = units
    for h in range(lags.shape[0]):
        plan[LAG + h] = 2 * lags[h]
        for p in range(pairs.shape[1]):
            weights[p * lags.shape[0] + h] = table[rows[p], h]


def launch(kernel, inputs, outputs, scratch, earlier, aliases=None):
    begin, end = len(inputs), len(inputs) + len(earlier)

    def body(*refs):
        results = refs[end : end + len(outputs)]
        token = refs[end + len(outputs)]
        kernel(*refs[:begin], *results, *refs[end + len(outputs) + 1 :])
        token[...] = jnp.zeros_like(token)

    return pl.pallas_call(
        body,
        out_shape=[shape for shape, _ in outputs] + [jax.ShapeDtypeStruct((8, 128), F32)],
        in_specs=[memory for _, memory in inputs] + [HBM] * len(earlier),
        out_specs=[memory for _, memory in outputs] + [VMEM],
        scratch_shapes=scratch,
        input_output_aliases=aliases or {},
        compiler_params=pltpu.CompilerParams(vmem_limit_bytes=SCOPED),
        cost_estimate=pl.CostEstimate(flops=0, bytes_accessed=2000000, transcendentals=0),
    )(*[array for array, _ in inputs], *earlier)


def fetch(field, source, receiver, target, sem):
    snaps = receiver.shape[0]
    width = pl.ds(0, target.shape[-1])

    @pl.when(field < snaps)
    def _():
        pltpu.make_async_copy(receiver.at[jnp.minimum(field, snaps - 1), :, :, width], target, sem).start()

    @pl.when(field >= snaps)
    def _():
        pltpu.make_async_copy(source.at[jnp.maximum(field - snaps, 0), :, :, width], target, sem).start()

    return pltpu.make_async_copy(receiver.at[0, :, :, width], target, sem)


def lead_kernel(plan, source, receiver, out, sem):
    fetch(plan[FIELD], source, receiver, out, sem).wait()


def lead(plan, source, receiver, width):
    block = jax.ShapeDtypeStruct(source.shape[1:3] + (width,), F32)
    inputs = [(plan, SMEM), (source, HBM), (receiver, HBM)]
    return launch(lead_kernel, inputs, [(block, VMEM)], [pltpu.SemaphoreType.DMA], [])


def gather_kernel(plan, source, receiver, fields, inner, outer, sems):
    count, cells, rows, _ = fields.shape
    waits = [fetch(plan[FIELD + s], source, receiver, fields.at[s], sems.at[s]) for s in range(count)]
    second = plan[SECOND] == 1
    for s, wait in enumerate(waits):
        wait.wait()

        def rim(x, carry):
            low, high = fields[s, x, 0:2], fields[s, x, rows - 2 : rows]
            inner[s, x] = jnp.where(second, low, high)
            outer[s, x] = jnp.where(second, high, low)
            return carry

        lax.fori_loop(0, cells, rim, 0, unroll=4)


def gather(plan, source, receiver, count, earlier):
    _, cells, rows, depth = source.shape
    edge = jax.ShapeDtypeStruct((count, cells, 2, depth), F32)
    whole = jax.ShapeDtypeStruct((count, cells, rows, depth), F32)
    inputs = [(plan, SMEM), (source, HBM), (receiver, HBM)]
    outputs = [(whole, VMEM), (edge, VMEM), (edge, VMEM)]
    return launch(gather_kernel, inputs, outputs, [pltpu.SemaphoreType.DMA((count,))], earlier)


def take_kernel(piece, fields, out, sem):
    slot, start, width = piece
    copy = pltpu.make_async_copy(fields.at[slot, :, :, pl.ds(start, width)], out, sem)
    copy.start()
    copy.wait()


def take(piece, fields, earlier):
    block = jax.ShapeDtypeStruct(fields.shape[1:3] + piece[2:], F32)
    kernel = functools.partial(take_kernel, piece)
    return launch(kernel, [(fields, HBM)], [(block, VMEM)], [pltpu.SemaphoreType.DMA], earlier)


def turn_kernel(piece, block, fields, same, out, sem):
    take_kernel(piece, fields, out, sem)


def turn(block, piece, fields, earlier):
    shape = jax.ShapeDtypeStruct(block.shape, F32)
    out = jax.ShapeDtypeStruct(fields.shape[1:3] + piece[2:], F32)
    kernel = functools.partial(turn_kernel, piece)
    outputs = [(shape, HBM), (out, VMEM)]
    return launch(kernel, [(block, HBM), (fields, HBM)], outputs, [pltpu.SemaphoreType.DMA], earlier, {0: 0})


def gate_kernel(block, same):
    pass


def gate(block, earlier):
    shape = jax.ShapeDtypeStruct(block.shape, F32)
    return launch(gate_kernel, [(block, HBM)], [(shape, HBM)], [], earlier, {0: 0})


def cut_kernel(many, plan, *rest):
    blocks, inner = rest[:many], rest[many]
    cells, rows, _ = blocks[0].shape
    second = plan[SECOND] == 1
    start = 0
    for block in blocks:
        lanes = slice(start, start + block.shape[2])
        start = lanes.stop

        def rim(x, carry):
            inner[x, :, lanes] = jnp.where(second, block[x, 0:2], block[x, rows - 2 : rows])
            return carry

        lax.fori_loop(0, cells, rim, 0, unroll=4)


def cut_type(blocks):
    return jax.ShapeDtypeStruct((blocks[0].shape[0], 2, sum(block.shape[2] for block in blocks)), F32)


def cut(plan, blocks, earlier):
    inputs = [(plan, SMEM)] + [(block, VMEM) for block in blocks]
    return launch(functools.partial(cut_kernel, len(blocks)), inputs, [(cut_type(blocks), VMEM)], [], earlier)


def cut_all_kernel(plan, inner, block, out, sem):
    count, rows = inner.shape[0], block.shape[1]
    copy = pltpu.make_async_copy(inner, out.at[pl.ds(0, count)], sem)
    copy.start()
    second = plan[SECOND] == 1

    def rim(x, carry):
        out[count, x] = jnp.where(second, block[x, 0:2], block[x, rows - 2 : rows])
        return carry

    lax.fori_loop(0, block.shape[0], rim, 0, unroll=4)
    copy.wait()


def cut_all(plan, inner, block, earlier):
    edge = jax.ShapeDtypeStruct((inner.shape[0] + 1,) + inner.shape[1:], F32)
    inputs = [(plan, SMEM), (inner, VMEM), (block, VMEM)]
    return launch(cut_all_kernel, inputs, [(edge, VMEM)], [pltpu.SemaphoreType.DMA], earlier)


def image_kernel(
    piece, spot, plan, weights, fields, near, far, own_twin, own_edge, near_twin, near_edge, far_twin, far_edge, *rest
):
    to_source, to_receiver, ext, prod, mix, mext, done, sems = rest[-8:]
    slot, start, _ = piece
    _, cells, rows, _ = fields.shape
    halves, lanes = ext.shape[0], ext.shape[3]
    pairs = to_source.shape[0]
    taps = weights.shape[0] // pairs
    odd, second = plan[ODD], plan[SECOND] == 1
    near_at = jnp.where(odd == 1, 0, 2 * cells)
    far_at = 2 * cells - near_at
    first, last = plan[FIRST + slot], plan[FIRST + slot + 1]
    part = [slice(z * lanes, (z + 1) * lanes) for z in range(halves)]
    whole = [slice(start + z * lanes, start + (z + 1) * lanes) for z in range(halves)]
    passed = [slice(spot + z * lanes, spot + (z + 1) * lanes) for z in range(halves)]
    low_tile = lax.broadcasted_iota(jnp.int32, (8, lanes), 0)

    def widen(target, at, block, block_lanes, twin, twin_lanes, edge):
        def one(x, carry):
            for z in range(halves):
                t, e = twin[x, :, twin_lanes[z]], edge[x, :, whole[z]]
                target[z, at + x, 8 : rows + 8] = block[x, :, block_lanes[z]]
                target[z, at + x, 6:8] = jnp.where(second, t, e)
                target[z, at + x, rows + 8 : rows + 10] = jnp.where(second, e, t)
            return carry

        lax.fori_loop(0, cells, one, 0, unroll=4)

    widen(ext, cells, fields.at[slot], whole, own_twin.at[slot], whole, own_edge.at[slot])
    near_twin = near_twin.at[near_twin.shape[0] - 1] if len(near_twin.shape) == 4 else near_twin
    widen(ext, near_at, near, part, near_twin, part, near_edge.at[slot])
    widen(ext, far_at, far, part, far_twin, passed, far_edge.at[slot])

    def product(x, carry):
        for z in range(halves):
            e, q = ext.at[z, x], prod.at[z, x]
            here = e[8 : rows + 8]
            q[0:rows] = here * here
            q[rows : 2 * rows] = here * e[9 : rows + 9]
            q[2 * rows : 3 * rows] = here * e[10 : rows + 10]
            base = e[0:8]
            one = base * e[1:9]
            two = base * e[2:10]
            q[3 * rows : 3 * rows + 8] = jnp.where(low_tile >= 6, two, pltpu.roll(one, 6, 0))
        return carry

    lax.fori_loop(0, 3 * cells, product, 0, unroll=4)

    def window(target, p):
        return target.at[p, :, :, pl.ds(start, halves * lanes)]

    def unit(index, carry):
        i = index - first
        u = plan[ORDER + index]
        to_r = lax.rem(u, 2)
        p = lax.div(u, 2)
        mate = plan[SLOT + u + 1 - 2 * to_r]
        sign = 1 - 2 * to_r
        at = [cells + sign * plan[LAG + h] for h in range(taps)]
        scale = [weights[p * taps + h] for h in range(taps)]
        widen(mext, 0, fields.at[mate], whole, own_twin.at[mate], whole, own_edge.at[mate])

        def total(x, carry):
            for z in range(halves):
                m, s = mix.at[z], mext.at[z, x]
                acc = None
                for h in range(taps):
                    term = scale[h] * prod[z, x + at[h]]
                    acc = term if acc is None else acc + term
                m[0, 8 : rows + 8] = acc[rows : 2 * rows]
                m[1, 8 : rows + 8] = acc[2 * rows : 3 * rows]
                extra = acc[3 * rows : 3 * rows + 8]
                m[0, 0:8] = pltpu.roll(extra, 2, 0)
                m[1, 0:8] = extra
                one = acc[rows : 2 * rows] * s[9 : rows + 9] + m[0, 7 : rows + 7] * s[7 : rows + 7]
                two = acc[2 * rows : 3 * rows] * s[10 : rows + 10] + m[1, 6 : rows + 6] * s[6 : rows + 6]
                done[i, x, :, part[z]] = 0.375 * (acc[0:rows] * s[8 : rows + 8]) + 0.25 * one + 0.0625 * two
            return carry

        lax.fori_loop(0, cells, total, 0)
        for which, target in enumerate((to_source, to_receiver)):

            @pl.when(to_r == which)
            def _():
                pltpu.make_async_copy(done.at[i], window(target, p), sems.at[i]).start()

        return carry

    lax.fori_loop(first, last, unit, 0)

    def settle(index, carry):
        i = index - first
        pltpu.make_async_copy(done.at[i], window(to_source, 0), sems.at[i]).wait()
        return carry

    lax.fori_loop(first, last, settle, 0)


def joint_kernel(many, piece, spot, news, *refs):
    plan, blocks, begin = refs[0], refs[1 : 1 + many], 1 + many
    results = refs[begin + 10 + news :]
    if many:
        cut_kernel(many, plan, *blocks, results[0])
        results = results[1:]
    image_kernel(piece, spot, plan, *refs[begin : begin + 10], *results)


def image(blocks, piece, pairs, plan, weights, fields, near, far, halos, spot, outs, earlier):
    _, cells, rows, depth = fields.shape
    whole = jax.ShapeDtypeStruct((pairs, cells, rows, depth), F32)
    lanes = 128 if piece[2] % 128 == 0 else piece[2]
    halves = piece[2] // lanes
    inputs = [(plan, SMEM)] + [(block, VMEM) for block in blocks]
    inputs += [(weights, SMEM), (fields, VMEM), (near, VMEM), (far, VMEM)] + [(halo, VMEM) for halo in halos]
    first = len(inputs)
    inputs += [(out, HBM) for out in outs]
    outputs = ([(cut_type(blocks), VMEM)] if blocks else []) + [(whole, HBM), (whole, HBM)]
    scratch = [
        pltpu.VMEM((halves, 3 * cells, rows + 16, lanes), F32),
        pltpu.VMEM((halves, 3 * cells, 3 * rows + 8, lanes), F32),
        pltpu.VMEM((halves, 2, rows + 8, lanes), F32),
        pltpu.VMEM((halves, cells, rows + 16, lanes), F32),
        pltpu.VMEM((pairs, cells, rows, halves * lanes), F32),
        pltpu.SemaphoreType.DMA((pairs,)),
    ]
    kernel = functools.partial(joint_kernel, len(blocks), piece, spot, len(outs))
    aliases = {first + i: len(outputs) - 2 + i for i in range(len(outs))}
    return launch(kernel, inputs, outputs, scratch, earlier, aliases)


AHEAD, TWINS = 2, 1
SOON, JOINED = (4,), (5,)
def pieces_of(count, depth):
    return [(slot, 0, depth) for slot in range(count)]


def work(count, pairs, routes, plan, weights, source, receiver):
    send = lambda value, route: lax.ppermute(value, ("gx", "gy"), routes[route])
    pieces = pieces_of(count, source.shape[3])
    last = len(pieces)

    first, token = lead(plan, source, receiver, pieces[0][2])
    near = [send(first, "across")]
    fields, inner, outer, token = gather(plan, source, receiver, count, [token])
    own_twin = None if count in JOINED else send(inner, "twins")
    earlier = []
    for piece in pieces[1:AHEAD]:
        block, token = take(piece, fields, [token] + earlier)
        near.append(send(block, "across"))
        earlier = []
    outer, token = gate(outer, [token])
    near_edge = send(outer, "seam_near")
    far_edge = send(outer, "seam_far")
    own_edge = send(outer, "seam")

    def needed(k):
        soon = [near_edge, far_edge] + ([] if count in JOINED else [own_twin]) + ([own_edge] if count in SOON else [])
        return soon if k == 1 else [own_edge]

    far, twins, outs = [], [], ()

    def sums(blocks, k, outs, token):
        halos = (twins[0] if count in JOINED else own_twin, own_edge, twins[k], near_edge, twins[k + 1], far_edge)
        spot = pieces[k + 1][2] if k + 1 < last else 0
        *edge, to_source, to_receiver, token = image(
            blocks, pieces[k], pairs, plan, weights, fields, near[k], far[k], halos, spot, outs, [token]
        )
        return edge, (to_source, to_receiver), token

    for k in range(last):
        earlier = [token] + (twins[k - TWINS : k - TWINS + 1] if TWINS <= k else []) + (needed(k) if k in (1, 2) else [])
        if k + AHEAD < last:
            near[k], block, token = turn(near[k], pieces[k + AHEAD], fields, earlier)
            near.append(send(block, "across"))
        else:
            near[k], token = gate(near[k], earlier)
        far.append(send(near[k], "onward"))
        blocks = near[k : k + 1] + (far[k - 1 : k] if k >= 1 else [])
        if k < 2:
            edge, token = cut_all(plan, inner, near[0], [token]) if k == 0 and count in JOINED else cut(plan, blocks, [token])
        else:
            (edge,), outs, token = sums(blocks, k - 2, outs, token)
        twins.append(send(edge, "twins"))
    _, outs, token = sums([], last - 2, outs, token)
    edge, token = cut(plan, far[last - 1 :], [token])
    twins.append(send(edge, "twins"))
    _, outs, token = sums([], last - 1, outs, token)
    return outs


def local(routes, source_snaps, receiver_snaps, snap_pairs, offset_lags, weight_table, weight_index):
    pairs = snap_pairs.shape[0]
    least, most = 2, 2 * pairs
    plan, weights, branch = pl.pallas_call(
        functools.partial(plan_kernel, receiver_snaps.shape[0], least),
        out_shape=[
            jax.ShapeDtypeStruct((LAG + offset_lags.shape[0],), jnp.int32),
            jax.ShapeDtypeStruct((pairs * offset_lags.shape[0],), F32),
            jax.ShapeDtypeStruct((1,), jnp.int32),
        ],
        in_specs=[SMEM] * 4,
        out_specs=[SMEM] * 3,
    )(snap_pairs.T, offset_lags, weight_table, weight_index)
    branches = [functools.partial(work, count, pairs, routes) for count in range(least, most + 1)]
    return lax.switch(branch[0], branches, plan, weights, source_snaps, receiver_snaps)


def solution(mesh):
    routes = moves(mesh)
    split = P(None, "gx", "gy", None)
    return jax.shard_map(
        functools.partial(local, routes),
        mesh=mesh,
        in_specs=(split, split, P(), P(), P(), P()),
        out_specs=(split, split),
        check_vma=False,
    )
```
